32 devices in a mesh: slab: 8 (over z, x), xy: 4 (over y, core).
Axes of the slice: x: 2, y: 2, z: 4, core: 2. Of those that a mesh axis runs over, the one named last changes fastest.
Arguments:
- atom_feats: bfloat16 [2048, 16, 128], P(('slab', 'xy')), may hold values from -6 to 6
- mix_weight: bfloat16 [4, 128, 128], replicated, may hold values from -0.5 to 0.5
- gate_weight: bfloat16 [128, 384], replicated, may hold values from -0.5 to 0.5
- radial_weight: float32 [8, 512], replicated, may hold values from -2 to 2
- out_weight: float32 [128], replicated, may hold values from -0.5 to 0.5
- pair_vec: float32 [3, 8, 4096], P(None, None, ('slab', 'xy')), may hold values from -1.5 to 1.5
- nbr_atom: int32 [8, 4096], P(None, ('slab', 'xy')), may hold values from 0 to 2047, as said below
- nbr_count: int32 [4096], P(('slab', 'xy')), may hold values from 1 to 8
- target: float32 [4096], P(('slab', 'xy')), may hold values from -6 to 6
Outputs:
- density: float32 [4096], P(('slab', 'xy'))
- feat_grad: float32 [2048, 16, 128], P(('slab', 'xy'))
- mix_grad: float32 [4, 128, 128], replicated
- gate_grad: float32 [128, 384], replicated
The draws below stay inside these ranges and needn't reach their ends.
Inputs may be any that keep to these rules, and one draw needn't show every extreme that they name: `nbr_atom`: atom numbers run domain by domain, 64 atoms each, domains in the order of the probes' slabs. Every entry of a probe's block, live or padding, names an atom of a domain in the probe's own z slab or in the z slab just below or above it (any in-plane position); one from the slab below is among the last 16 atoms of its domain, one from the slab above among the first 16.
All inputs are finite; a program needn't handle non-finite values.
Results may differ from the reference program's by a relative error of at most 0.003.
Values may be sent and summed in bfloat16 or wider, within the bound.
No kernel may reach another device: no remote copies, remote signals or barrier semaphores. Data moves between devices by JAX's collectives and lax.ppermute only.
A program may use at most 64 MiB of HBM per device.

```python
import math
import jax
import jax.numpy as jnp
import numpy as np
from jax import lax

C = 128
HARM = 16
B = 8
K = 8
ATOM_DEV = 64
PROBE_DEV = 128
RIM = 16
ATOMS = 2048
PROBES = 4096
N_SLAB = 8
N_XY = 4


def draw_nbr_atom(key, part):
    key_slab = jax.random.fold_in(key, 11)
    key_plane = jax.random.fold_in(key, 12)
    key_row = jax.random.fold_in(key, 13)
    probe_ids = jnp.arange(PROBES, dtype=jnp.int32)
    slab_of = probe_ids // PROBE_DEV // N_XY
    offsets = jax.random.randint(key_slab, (K, PROBES), -1, 2, dtype=jnp.int32)
    target_slab = jnp.clip(slab_of[None, :] + offsets, 0, N_SLAB - 1)
    step_slab = target_slab - slab_of[None, :]
    plane = jax.random.randint(key_plane, (K, PROBES), 0, N_XY, dtype=jnp.int32)
    raw_row = jax.random.randint(key_row, (K, PROBES), 0, ATOM_DEV, dtype=jnp.int32)
    row_pick = jnp.where(step_slab == -1, ATOM_DEV - RIM + raw_row % RIM, jnp.where(step_slab == 1, raw_row % RIM, raw_row))
    return ((target_slab * N_XY + plane) * ATOM_DEV + row_pick).astype(jnp.int32)


def plant(values, key, smallest, top_value):
    place = [jax.random.randint(jax.random.fold_in(key, axis), (), 0, length) for axis, length in enumerate(values.shape)]
    main_axis = values.shape.index(max(values.shape))
    beside = place[:main_axis] + [(place[main_axis] + 1) % values.shape[main_axis]] + place[main_axis + 1:]
    return values.at[tuple(place)].set(smallest).at[tuple(beside)].set(top_value)


def steps_of(stream_key, shape, split, least, largest):
    loudness = 1.0
    for axis_at, blocks in split:
        steps = jax.random.uniform(jax.random.fold_in(jax.random.fold_in(stream_key, 6), axis_at), (blocks,), jnp.float32, least / len(split), largest / len(split))
        loudness = loudness * jnp.repeat(jnp.exp(steps), shape[axis_at] // blocks).reshape((-1,) + (1,) * (len(shape) - 1 - axis_at))
    return loudness


def noise(rng, shape, scale, most, shards=(), kind=jnp.bfloat16):
    result = jax.random.normal(rng, shape, jnp.float32) * scale
    if len(shards) > 0:
        result = steps_of(rng, shape, shards, -0.22, 0.18) * result
    return jnp.clip(result, min=-most, max=most).astype(kind)


def setup_inputs(seed: int = 0) -> dict:
    streams_of = jax.random.split(jax.random.key(seed), 10)
    return {
        "atom_feats": noise(streams_of[0], (ATOMS, HARM, C), 1.0, 6.0, ((0, 32),)),
        "mix_weight": noise(streams_of[1], (4, C, C), C ** -0.5, 0.5),
        "gate_weight": noise(streams_of[2], (C, 3 * C), C ** -0.5, 0.5),
        "radial_weight": noise(streams_of[3], (B, 4 * C), B ** -0.5, 2.0, (), jnp.float32),
        "out_weight": noise(streams_of[4], (C,), C ** -0.5, 0.5, (), jnp.float32),
        "pair_vec": jnp.clip(jax.random.uniform(streams_of[5], (3, K, PROBES), jnp.float32, -1.5, 1.5) * steps_of(streams_of[5], (3, K, PROBES), ((2, 32),), -0.4, 0.0), -1.5, 1.5),
        "nbr_atom": draw_nbr_atom(jax.random.fold_in(streams_of[9], 71), 0),
        "nbr_count": plant(jax.random.randint(streams_of[7], (PROBES,), 1, K + 1), jax.random.fold_in(streams_of[7], 1), 1, K).astype(jnp.int32),
        "target": noise(streams_of[8], (PROBES,), 1.0, 6.0, ((0, 32),), jnp.float32),
    }


DEGREE_SPANS = ((0, 1), (1, 4), (4, 9), (9, 16))
DEGREE_REPEATS = (1, 3, 5, 7)
root_three = math.sqrt(3.0)
cubic_outer = math.sqrt(10.0) / 4.0
cubic_middle = math.sqrt(15.0)
cubic_inner = math.sqrt(6.0) / 4.0

def harmonics(vectors):
    along_x, along_y, along_z = (vectors[0], vectors[1], vectors[2])
    radius_sq = along_x * along_x + along_y * along_y + along_z * along_z
    terms = [jnp.ones_like(along_x), along_x, along_y, along_z, root_three * along_x * along_y, root_three * along_y * along_z, 0.5 * (3.0 * along_z * along_z - radius_sq), root_three * along_x * along_z, 0.5 * root_three * (along_x * along_x - along_y * along_y), cubic_outer * along_y * (3.0 * along_x * along_x - along_y * along_y), cubic_middle * along_x * along_y * along_z, cubic_inner * along_y * (5.0 * along_z * along_z - radius_sq), 0.5 * along_z * (5.0 * along_z * along_z - 3.0 * radius_sq), cubic_inner * along_x * (5.0 * along_z * along_z - radius_sq), 0.5 * cubic_middle * along_z * (along_x * along_x - along_y * along_y), cubic_outer * along_x * (along_x * along_x - 3.0 * along_y * along_y)]
    return (jnp.stack(terms, axis=0), radius_sq)

def pair_coefficient(vectors, radial_weight):
    harm_values, radius_sq = harmonics(vectors)
    nbasis = radial_weight.shape[0]
    hidden_widths = radial_weight.shape[1] // 4
    distance = jnp.sqrt(radius_sq)
    envelope = (1.0 - radius_sq / 7.0) ** 2
    centers = 0.35 * jnp.arange(nbasis, dtype=jnp.float32)
    basis = jnp.exp(-((distance[None, :] - centers[:, None]) / 0.35) ** 2) * envelope[None, :]
    radial = jnp.dot(basis.T, radial_weight, precision=lax.Precision.HIGHEST)
    radial = radial.reshape(radial.shape[0], 4, hidden_widths)
    expanded = jnp.repeat(radial, np.array(DEGREE_REPEATS), axis=1, total_repeat_length=16)
    return harm_values.T[:, :, None] * expanded

def silu_slope(values):
    sig = jax.nn.sigmoid(values)
    return sig * (1.0 + values * (1.0 - sig))

def atom_layer(features, mix_weight, gate_weight):
    hidden_widths = features.shape[2]
    count_atoms = features.shape[0]
    gate_pre = jnp.dot(features[:, 0, :], gate_weight, preferred_element_type=jnp.float32)
    gates = jax.nn.sigmoid(gate_pre)
    mixed = []
    updates = []
    for degree in range(4):
        start_row, end_row = DEGREE_SPANS[degree]
        block = features[:, start_row:end_row, :].reshape(-1, hidden_widths)
        product = jnp.dot(block, mix_weight[degree], preferred_element_type=jnp.float32)
        product = product.reshape(count_atoms, end_row - start_row, hidden_widths)
        mixed.append(product)
        if degree == 0:
            updates.append(jax.nn.silu(product))
        else:
            gate_block = gates[:, None, (degree - 1) * hidden_widths:degree * hidden_widths]
            updates.append(product * gate_block)
    atom_out = (features.astype(jnp.float32) + jnp.concatenate(updates, axis=1)).astype(jnp.bfloat16)
    return (atom_out, gates, mixed)

def layer_backward(features, mix_weight, gate_weight, gates, mixed, upstream):
    hidden_widths = features.shape[2]
    count_atoms = features.shape[0]
    wide = features.astype(jnp.float32)
    grad_blocks = []
    mix_grads = []
    gate_parts = []
    for degree in range(4):
        start_row, end_row = DEGREE_SPANS[degree]
        incoming = upstream[:, start_row:end_row, :]
        if degree == 0:
            d_mixed = incoming * silu_slope(mixed[0])
        else:
            gate_block = gates[:, None, (degree - 1) * hidden_widths:degree * hidden_widths]
            d_mixed = incoming * gate_block
            gate_parts.append(lax.optimization_barrier(jnp.sum(incoming * mixed[degree], axis=1)))
        flat_grad = d_mixed.reshape(-1, hidden_widths)
        flat_feat = wide[:, start_row:end_row, :].reshape(-1, hidden_widths)
        mix_grads.append(jnp.dot(flat_feat.T, flat_grad, precision=lax.Precision.HIGHEST))
        back = jnp.dot(flat_grad, mix_weight[degree].astype(jnp.float32).T, precision=lax.Precision.HIGHEST)
        grad_blocks.append(incoming + back.reshape(count_atoms, end_row - start_row, hidden_widths))
    d_gate_pre = jnp.concatenate(gate_parts, axis=1) * gates * (1.0 - gates)
    gate_grad = jnp.dot(wide[:, 0, :].T, d_gate_pre, precision=lax.Precision.HIGHEST)
    scalar_back = jnp.dot(d_gate_pre, gate_weight.astype(jnp.float32).T, precision=lax.Precision.HIGHEST)
    grad_blocks[0] = grad_blocks[0] + scalar_back[:, None, :]
    return (jnp.concatenate(grad_blocks, axis=1), jnp.stack(mix_grads, axis=0), gate_grad)

def probe_forward(source, coordinates, vectors, counts, radial_weight, out_weight):
    capacity_total = coordinates.shape[0]
    sampler_total = coordinates.shape[1]
    hidden_widths = source.shape[2]

    def proceed_once(neighbor_signal, slot):
        rows = source[coordinates[slot]]
        coefficient = pair_coefficient(vectors[:, slot, :], radial_weight)
        active = (slot < counts).astype(jnp.float32)
        term = lax.optimization_barrier(jnp.sum(coefficient * rows.astype(jnp.float32), axis=1))
        return (neighbor_signal + active[:, None] * term, None)
    neighbor_signal, discarded_result = lax.scan(proceed_once, jnp.zeros((sampler_total, hidden_widths), jnp.float32), jnp.arange(capacity_total, dtype=jnp.int32))
    density = jnp.dot(jax.nn.silu(neighbor_signal), out_weight, precision=lax.Precision.HIGHEST)
    return (density, neighbor_signal)

def probe_backward(derivative_input, coordinates, vectors, counts, radial_weight, d_message):
    capacity_total = coordinates.shape[0]

    def proceed_once(accumulated, slot):
        coefficient = pair_coefficient(vectors[:, slot, :], radial_weight)
        active = (slot < counts).astype(jnp.float32)
        contribution = (active[:, None] * d_message)[:, None, :] * coefficient
        return (accumulated.at[coordinates[slot]].add(contribution), None)
    derivative_input, discarded_result = lax.scan(proceed_once, derivative_input, jnp.arange(capacity_total, dtype=jnp.int32))
    return derivative_input

def message_grad(density, neighbor_signal, targets, out_weight, probes_dev):
    d_density = (density - targets) / probes_dev
    return d_density[:, None] * out_weight[None, :] * silu_slope(neighbor_signal)

def reference(atom_feats, mix_weight, gate_weight, radial_weight, out_weight, pair_vec, nbr_atom, nbr_count, target):
    atom_out, gates, mixed = atom_layer(atom_feats, mix_weight, gate_weight)
    nblocks = PROBES // PROBE_DEV
    vec_blocks = jnp.moveaxis(pair_vec.reshape(3, K, nblocks, PROBE_DEV), 2, 0)
    idx_blocks = jnp.moveaxis(nbr_atom.reshape(K, nblocks, PROBE_DEV), 1, 0)
    count_blocks = nbr_count.reshape(nblocks, PROBE_DEV)
    target_blocks = target.reshape(nblocks, PROBE_DEV)

    def one_block(accumulated, inputs):
        vectors, coordinates, counts, targets = inputs
        density, neighbor_signal = probe_forward(atom_out, coordinates, vectors, counts, radial_weight, out_weight)
        d_message = message_grad(density, neighbor_signal, targets, out_weight, float(PROBE_DEV))
        accumulated = probe_backward(accumulated, coordinates, vectors, counts, radial_weight, d_message)
        return (accumulated, density)
    start = jnp.zeros(atom_out.shape, jnp.float32)
    upstream, densities = lax.scan(one_block, start, (vec_blocks, idx_blocks, count_blocks, target_blocks))
    feat_grad, mix_sum, gate_sum = layer_backward(atom_feats, mix_weight, gate_weight, gates, mixed, upstream)
    scale = 1.0 / float(N_SLAB * N_XY)
    return (densities.reshape(PROBES), feat_grad, mix_sum * scale, gate_sum * scale)
```

```python
import functools
import math

import jax
import jax.numpy as jnp
from jax import lax
from jax.experimental import pallas as pl
from jax.experimental.pallas import tpu as pltpu
from jax.sharding import PartitionSpec as P

DEGREE_SPANS = ((0, 1), (1, 4), (4, 9), (9, 16))
DEGREE_OF = (0,) + (1,) * 3 + (2,) * 5 + (3,) * 7
HARM = 16
SPACING = 0.35
root_three = math.sqrt(3.0)
cubic_outer = math.sqrt(10.0) / 4.0
cubic_middle = math.sqrt(15.0)
cubic_inner = math.sqrt(6.0) / 4.0
VMEM_BYTES = 56 * 2**20
F32 = jnp.float32
BF16 = jnp.bfloat16


def harmonics(x, y, z):
    r2 = x * x + y * y + z * z
    terms = [
        None,
        x,
        y,
        z,
        root_three * x * y,
        root_three * y * z,
        0.5 * (3.0 * z * z - r2),
        root_three * x * z,
        0.5 * root_three * (x * x - y * y),
        cubic_outer * y * (3.0 * x * x - y * y),
        cubic_middle * x * y * z,
        cubic_inner * y * (5.0 * z * z - r2),
        0.5 * z * (5.0 * z * z - 3.0 * r2),
        cubic_inner * x * (5.0 * z * z - r2),
        0.5 * cubic_middle * z * (x * x - y * y),
        cubic_outer * x * (x * x - 3.0 * y * y),
    ]
    return terms, r2


def split_high_low(values):
    high = values.astype(BF16)
    return high, (values - high.astype(F32)).astype(BF16)


def dot_lanes(left, right):
    return lax.dot_general(left, right, (((1,), (1,)), ((), ())), preferred_element_type=F32)


def dot(left, right):
    return jnp.dot(left, right, preferred_element_type=F32)


def partner(block, axis, bit):
    count = lax.axis_size(axis)
    return lax.ppermute(block, axis, [(i, i ^ bit) for i in range(count)])


def shifted(block, axis, step):
    count = lax.axis_size(axis)
    return lax.ppermute(block, axis, [(i, i + step) for i in range(count) if 0 <= i + step < count])


class Pairs:
    def __init__(self, info, slots, atoms, face_rows, plane, me):
        def rows(first):
            return jnp.concatenate([ref[first * slots : (first + 1) * slots, :] for ref in info], axis=1)

        self.slots = slots
        self.harm, r2 = harmonics(rows(0), rows(1), rows(2))
        code = rows(3).astype(jnp.int32)
        tail = rows(4)
        slot = lax.broadcasted_iota(jnp.int32, code.shape, 0).astype(F32)
        active = (slot < tail[0:1, :]).astype(F32)
        self.target = tail[1:2, :]
        relative = (code & (plane - 1)) ^ me
        offset = code >> (plane.bit_length() - 1)
        width = jnp.where(offset < plane * atoms, atoms, 2 * face_rows)
        self.column = offset + relative * width
        envelope = (1.0 - r2 / 7.0) ** 2 * active
        self.basis_parts = (jnp.sqrt(r2), envelope)

    def radial(self, lhs_ref, out_ref, nbasis):
        distance, envelope = self.basis_parts
        values = [
            jnp.exp(-(((distance - SPACING * b) / SPACING) ** 2)) * envelope for b in range(nbasis)
        ]
        basis = jnp.concatenate(values, axis=0)
        high, low = split_high_low(basis)
        stack = jnp.concatenate([high, low, high], axis=0)
        out_ref[...] = dot(lhs_ref[...], stack)

    def table(self, k, total):
        column = self.column[k : k + 1, :]
        rows = lax.broadcasted_iota(jnp.int32, (total, column.shape[1]), 0)
        return jnp.where(rows == column, 1.0, 0.0).astype(BF16)

    def weight(self, lm, k):
        return self.harm[lm][k : k + 1, :]


def forward_kernel(slots, plane, me_ref, *refs):
    wide = refs[:plane]
    faces = refs[plane : 2 * plane]
    info = refs[2 * plane : 3 * plane]
    mix_ref, gate_ref, radial_ref, out_w_ref = refs[3 * plane : 3 * plane + 4]
    feats_ref, mixed_ref, gates_ref, msg_ref, dens_ref = refs[3 * plane + 4 : 3 * plane + 9]
    table_ref, coef_ref = refs[3 * plane + 9 :]
    atoms = wide[0].shape[1]
    edge = faces[0].shape[1]
    total = plane * (atoms + edge)
    part = mix_ref.shape[1] // 2
    for j in range(plane):
        feats_ref[:, j * atoms : (j + 1) * atoms, :] = wide[j][...]
        feats_ref[:, plane * atoms + j * edge : plane * atoms + (j + 1) * edge, :] = faces[j][...]
    gates_ref[...] = jax.nn.sigmoid(dot_lanes(gate_ref[...], feats_ref[0]))
    for lm in range(HARM):
        degree = DEGREE_OF[lm]
        both = dot_lanes(mix_ref[degree], feats_ref[lm])
        mixed, plain = both[:part], both[part:]
        mixed_ref[lm * part : (lm + 1) * part, :] = mixed
        if degree == 0:
            update = mixed * jax.nn.sigmoid(mixed)
        else:
            update = mixed * gates_ref[(degree - 1) * part : degree * part, :]
        table_ref[lm * part : (lm + 1) * part, :] = (plain + update).astype(BF16)
    pairs = Pairs(info, slots, atoms, edge // 2, plane, me_ref[0])
    nbasis = radial_ref.shape[1] // (3 * slots)
    pairs.radial(radial_ref, coef_ref, nbasis)
    message = jnp.zeros(msg_ref.shape, F32)
    for k in range(slots):
        rows = dot(table_ref[...], pairs.table(k, total))
        for degree, (start, end) in enumerate(DEGREE_SPANS):
            inner = None
            for lm in range(start, end):
                term = rows[lm * part : (lm + 1) * part]
                if lm > 0:
                    term = term * pairs.weight(lm, k)
                inner = term if inner is None else inner + term
            at = (k * 4 + degree) * part
            message = message + inner * coef_ref[at : at + part, :]
    msg_ref[...] = message
    partial = jnp.sum(message * jax.nn.sigmoid(message) * out_w_ref[...], axis=0, keepdims=True)
    dens_ref[...] = jnp.broadcast_to(partial, dens_ref.shape)


def backward_kernel(slots, plane, scale, probes_dev, me_ref, *refs):
    info = refs[:plane]
    dens = refs[plane : 2 * plane]
    feats_ref, mixed_ref, gates_ref, msg_ref, radial_ref, out_w_ref = refs[2 * plane : 2 * plane + 6]
    weight_ref, density_ref = refs[2 * plane + 6 : 2 * plane + 8]
    send_refs = refs[2 * plane + 8 : 3 * plane + 8]
    coef_ref, grad_ref = refs[3 * plane + 8 :]
    part = msg_ref.shape[0]
    total = feats_ref.shape[1]
    rows_out = send_refs[0].shape[0]
    atoms = 2 * rows_out // 3
    edge = rows_out - atoms
    probes = msg_ref.shape[1] // plane
    pairs = Pairs(info, slots, atoms, edge // 2, plane, me_ref[0])
    pairs.radial(radial_ref, coef_ref, radial_ref.shape[1] // (3 * slots))
    density = dens[0][0:1, :]
    for j in range(1, plane):
        other = dens[j][0:1, :]
        density = density + jnp.concatenate(
            [other[:, (b ^ j) * probes : ((b ^ j) + 1) * probes] for b in range(plane)], axis=1
        )
    density_ref[...] = jnp.broadcast_to(density[:, :probes], density_ref.shape)
    d_density = (density - pairs.target) * (1.0 / probes_dev)
    message = msg_ref[...]
    sig = jax.nn.sigmoid(message)
    d_message = d_density * out_w_ref[...] * (sig * (1.0 + message * (1.0 - sig)))
    for k in range(slots):
        pieces = []
        for degree, (start, end) in enumerate(DEGREE_SPANS):
            at = (k * 4 + degree) * part
            base = coef_ref[at : at + part, :] * d_message
            for lm in range(start, end):
                piece = base if lm == 0 else base * pairs.weight(lm, k)
                pieces.append(piece.astype(BF16))
        contribution = jnp.concatenate(pieces, axis=0)
        product = dot_lanes(contribution, pairs.table(k, total))
        if k == 0:
            grad_ref[...] = product
        else:
            grad_ref[...] += product
    for degree, (start, end) in enumerate(DEGREE_SPANS):
        sums = None
        gate_sum = None
        for lm in range(start, end):
            grad = grad_ref[lm * part : (lm + 1) * part, :]
            mixed = mixed_ref[lm * part : (lm + 1) * part, :]
            if degree == 0:
                s = jax.nn.sigmoid(mixed)
                d_mixed = grad * (s * (1.0 + mixed * (1.0 - s)))
            else:
                d_mixed = grad * gates_ref[(degree - 1) * part : degree * part, :]
                gate_sum = grad * mixed if gate_sum is None else gate_sum + grad * mixed
            high, low = split_high_low(d_mixed)
            product = dot(jnp.concatenate([high, low], axis=0), feats_ref[lm])
            sums = product if sums is None else sums + product
        weight_ref[degree * part : (degree + 1) * part, :] = (sums[:part] + sums[part:]) * scale
        if degree > 0:
            gates = gates_ref[(degree - 1) * part : degree * part, :]
            high, low = split_high_low(gate_sum * gates * (1.0 - gates))
            product = dot(jnp.concatenate([high, low], axis=0), feats_ref[0])
            at = (3 + degree) * part
            weight_ref[at : at + part, :] = (product[:part] + product[part:]) * scale
    turned = grad_ref[...].T
    for j in range(plane):
        send_refs[j][:atoms, :] = turned[j * atoms : (j + 1) * atoms].astype(BF16)
        at = plane * atoms + j * edge
        send_refs[j][atoms:, :] = turned[at : at + edge].astype(BF16)


def finish_kernel(plane, me_ref, *refs):
    slices = refs[:plane]
    below_ref, above_ref, feats_ref, mix_ref, gate_ref, out_ref = refs[plane:]
    atoms = feats_ref.shape[1]
    channels = feats_ref.shape[2]
    part = channels // plane
    face = below_ref.shape[1]
    per = channels // part
    me = me_ref[0]
    lane = lax.broadcasted_iota(jnp.int32, (atoms, channels), 1)
    gates = jax.nn.sigmoid(dot(feats_ref[0], gate_ref[...]))

    def slab(j, group):
        columns = slice(group * channels, (group + 1) * channels)
        own = slices[j][:atoms, columns].astype(F32)
        low = own[:face] + below_ref[j, :, columns].astype(F32)
        high = own[atoms - face :] + above_ref[j, :, columns].astype(F32)
        return jnp.concatenate([low, own[face : atoms - face], high], axis=0)

    upstream = []
    for group in range(HARM // per):
        blocks = [slab(j, group) for j in range(plane)]
        for place in range(per):
            total = None
            for j in range(plane):
                home = (me ^ j) * part
                shift = (home - place * part + channels) % channels
                moved = pltpu.roll(blocks[j], shift, 1)
                keep = jnp.where((lane >= home) & (lane < home + part), moved, 0.0)
                total = keep if total is None else total + keep
            upstream.append(total)
    gate_parts = []
    zero_row = None
    for degree, (start, end) in enumerate(DEGREE_SPANS):
        weight = mix_ref[degree]
        gate_sum = None
        for lm in range(start, end):
            mixed = dot(feats_ref[lm], weight)
            if degree == 0:
                s = jax.nn.sigmoid(mixed)
                d_mixed = upstream[lm] * (s * (1.0 + mixed * (1.0 - s)))
            else:
                d_mixed = upstream[lm] * gates[:, (degree - 1) * channels : degree * channels]
                product = upstream[lm] * mixed
                gate_sum = product if gate_sum is None else gate_sum + product
            high, low = split_high_low(d_mixed)
            back = dot_lanes(jnp.concatenate([high, low], axis=0), weight)
            result = upstream[lm] + back[:atoms] + back[atoms:]
            if degree == 0:
                zero_row = result
            else:
                out_ref[:, lm, :] = result
        if degree > 0:
            gate_parts.append(gate_sum)
    d_gate = jnp.concatenate(gate_parts, axis=1) * gates * (1.0 - gates)
    high, low = split_high_low(d_gate)
    back = dot_lanes(jnp.concatenate([high, low], axis=0), gate_ref[...])
    out_ref[:, 0, :] = zero_row + back[:atoms] + back[atoms:]


def assemble_kernel(plane, me_ref, *refs):
    pieces = refs[:plane]
    mix_ref, gate_ref = refs[plane : plane + 2]
    (joined_ref,) = refs[plane + 2 :]
    part = pieces[0].shape[0] // 7
    channels = plane * part
    for j in range(plane):
        home = pl.multiple_of((me_ref[0] ^ j) * part, part)
        for block in range(7):
            joined_ref[block, pl.ds(home, part), :] = pieces[j][block * part : (block + 1) * part, :]
    for block in range(4):
        mix_ref[block] = joined_ref[block].T
    for block in range(3):
        gate_ref[:, block * channels : (block + 1) * channels] = joined_ref[4 + block].T


def call(kernel, outs, scratch, scalars, *arrays):
    vmem = pl.BlockSpec(memory_space=pltpu.VMEM)
    return pl.pallas_call(
        kernel,
        out_shape=outs,
        in_specs=[pl.BlockSpec(memory_space=pltpu.SMEM)] + [vmem] * len(arrays),
        out_specs=jax.tree.map(lambda _: vmem, outs),
        scratch_shapes=scratch,
        compiler_params=pltpu.CompilerParams(vmem_limit_bytes=VMEM_BYTES),
    )(scalars, *arrays)


def body(
    atom_feats,
    mix_weight,
    gate_weight,
    radial_weight,
    out_weight,
    pair_vec,
    nbr_atom,
    nbr_count,
    target,
):
    atoms, harm_count, channels = atom_feats.shape
    slots, probes = nbr_atom.shape
    nbasis = radial_weight.shape[0]
    plane = lax.axis_size("xy")
    slabs = lax.axis_size("slab")
    part = channels // plane
    face = atoms // 4
    edge = 2 * face
    total = plane * (atoms + edge)
    lanes = plane * probes
    me = lax.axis_index("xy").astype(jnp.int32)
    me_arr = me[None]

    domain = nbr_atom // atoms
    row = nbr_atom % atoms
    step = domain // plane - lax.axis_index("slab")
    wide = plane * atoms
    offset = jnp.where(step == 0, row, jnp.where(step < 0, wide + row - (atoms - face), wide + face + row))
    code = offset * plane + domain % plane
    tail = jnp.concatenate(
        [nbr_count.astype(F32)[None], target[None], jnp.zeros((slots - 2, probes), F32)], axis=0
    )
    info = jnp.concatenate([pair_vec.reshape(3 * slots, probes), code.astype(F32), tail], axis=0)

    own = jnp.transpose(atom_feats, (1, 0, 2))
    from_below = shifted(own[:, atoms - face :, :], "slab", 1)
    from_above = shifted(own[:, :face, :], "slab", -1)
    faces = jnp.concatenate([from_below, from_above], axis=1)
    gathered = [(own, faces, info)]
    bits = [1 << b for b in reversed(range((plane - 1).bit_length()))]
    held = {0: (own, faces, info)}
    for bit in bits:
        for j in list(held):
            held[j ^ bit] = tuple(partner(x, "xy", bit) for x in held[j])
    pieces = [held[j] for j in range(plane)]

    first = me * part
    mix_part = lax.dynamic_slice_in_dim(mix_weight, first, part, axis=2)
    mix_part = jnp.transpose(mix_part, (0, 2, 1))
    pick = lax.broadcasted_iota(jnp.int32, (4, part, channels), 1) + first
    pick = (pick == lax.broadcasted_iota(jnp.int32, (4, part, channels), 2)).astype(BF16)
    mix_part = jnp.concatenate([mix_part, pick], axis=1)
    gate_part = lax.dynamic_slice_in_dim(gate_weight.reshape(channels, 3, channels), first, part, axis=2)
    gate_part = jnp.transpose(gate_part, (1, 2, 0)).reshape(3 * part, channels)
    radial_part = lax.dynamic_slice_in_dim(radial_weight.reshape(nbasis, 4, channels), first, part, axis=2)
    radial_part = jnp.transpose(radial_part, (1, 2, 0)).reshape(4 * part, nbasis)
    high = lax.reduce_precision(radial_part, 8, 7)
    three = jnp.stack([high, high, radial_part - high], axis=1)
    same = jnp.eye(slots, dtype=F32)
    radial_lhs = three[None, :, :, :, None] * same[:, None, None, None, :]
    radial_lhs = radial_lhs.reshape(slots * 4 * part, 3 * nbasis * slots).astype(BF16)
    out_part = lax.dynamic_slice_in_dim(out_weight, first, part)[:, None]

    infos = [p[2] for p in pieces]
    feats, mixed, gates, message, dens = call(
        functools.partial(forward_kernel, slots, plane),
        (
            jax.ShapeDtypeStruct((harm_count, total, channels), BF16),
            jax.ShapeDtypeStruct((harm_count * part, total), F32),
            jax.ShapeDtypeStruct((3 * part, total), F32),
            jax.ShapeDtypeStruct((part, lanes), F32),
            jax.ShapeDtypeStruct((8, lanes), F32),
        ),
        [
            pltpu.VMEM((harm_count * part, total), BF16),
            pltpu.VMEM((slots * 4 * part, lanes), F32),
        ],
        me_arr,
        *[p[0] for p in pieces],
        *[p[1] for p in pieces],
        *infos,
        mix_part,
        gate_part,
        radial_lhs,
        out_part,
    )
    dens_all = [dens] + [partner(dens, "xy", j) for j in range(1, plane)]

    outs = call(
        functools.partial(backward_kernel, slots, plane, 1.0 / float(slabs * plane), float(probes)),
        (
            jax.ShapeDtypeStruct((7 * part, channels), F32),
            jax.ShapeDtypeStruct((8, probes), F32),
        )
        + tuple(jax.ShapeDtypeStruct((atoms + edge, harm_count * part), BF16) for _ in range(plane)),
        [
            pltpu.VMEM((slots * 4 * part, lanes), F32),
            pltpu.VMEM((harm_count * part, total), F32),
        ],
        me_arr,
        *infos,
        *dens_all,
        feats,
        mixed,
        gates,
        message,
        radial_lhs,
        out_part,
    )
    weight, density, sends = outs[0], outs[1], list(outs[2:])

    have = {0: {j: sends[j] for j in range(plane)}}
    for bit in bits:
        fresh = {}
        for source, parts in have.items():
            fresh[source ^ bit] = {j ^ bit: partner(x, "xy", bit) for j, x in parts.items() if j & bit}
            have[source] = {j: x for j, x in parts.items() if not j & bit}
        have.update(fresh)
    slices = [have[j][0] for j in range(plane)]
    to_below = jnp.stack([s[atoms : atoms + face] for s in slices], axis=0)
    to_above = jnp.stack([s[atoms + face :] for s in slices], axis=0)
    grad_above = shifted(to_below, "slab", -1)
    grad_below = shifted(to_above, "slab", 1)
    feat_grad = call(
        functools.partial(finish_kernel, plane),
        jax.ShapeDtypeStruct((atoms, harm_count, channels), F32),
        [],
        me_arr,
        *slices,
        grad_below,
        grad_above,
        own,
        mix_weight,
        gate_weight,
    )

    for b in range((slabs - 1).bit_length()):
        weight = weight + partner(weight, "slab", 1 << b)
    columns = {0: weight}
    for bit in bits:
        for j in list(columns):
            columns[j ^ bit] = partner(columns[j], "xy", bit)
    mix_grad, gate_grad = call(
        functools.partial(assemble_kernel, plane),
        (
            jax.ShapeDtypeStruct((4, channels, channels), F32),
            jax.ShapeDtypeStruct((channels, 3 * channels), F32),
        ),
        [pltpu.VMEM((7, channels, channels), F32)],
        me_arr,
        *[columns[j] for j in range(plane)],
    )
    return (density[0], feat_grad, mix_grad, gate_grad)


def solution(mesh):
    in_specs = (
        P(("slab", "xy"), None, None),
        P(),
        P(),
        P(),
        P(),
        P(None, None, ("slab", "xy")),
        P(None, ("slab", "xy")),
        P(("slab", "xy")),
        P(("slab", "xy")),
    )
    out_specs = (P(("slab", "xy")), P(("slab", "xy"), None, None), P(), P())
    return jax.shard_map(body, mesh=mesh, in_specs=in_specs, out_specs=out_specs, check_vma=False)
```

```python
import functools
import math

import jax
import jax.numpy as jnp
from jax import lax
from jax.experimental import pallas as pl
from jax.experimental.pallas import tpu as pltpu
from jax.sharding import PartitionSpec as P

DEGREE_SPANS = ((0, 1), (1, 4), (4, 9), (9, 16))
DEGREE_OF = (0,) + (1,) * 3 + (2,) * 5 + (3,) * 7
HARM = 16
SPACING = 0.35
root_three = math.sqrt(3.0)
cubic_outer = math.sqrt(10.0) / 4.0
cubic_middle = math.sqrt(15.0)
cubic_inner = math.sqrt(6.0) / 4.0
VMEM_BYTES = 20 * 2**20
F32 = jnp.float32
BF16 = jnp.bfloat16


def harmonics(x, y, z):
    r2 = x * x + y * y + z * z
    terms = [
        None,
        x,
        y,
        z,
        root_three * x * y,
        root_three * y * z,
        0.5 * (3.0 * z * z - r2),
        root_three * x * z,
        0.5 * root_three * (x * x - y * y),
        cubic_outer * y * (3.0 * x * x - y * y),
        cubic_middle * x * y * z,
        cubic_inner * y * (5.0 * z * z - r2),
        0.5 * z * (5.0 * z * z - 3.0 * r2),
        cubic_inner * x * (5.0 * z * z - r2),
        0.5 * cubic_middle * z * (x * x - y * y),
        cubic_outer * x * (x * x - 3.0 * y * y),
    ]
    return terms, r2


def split_high_low(values):
    high = values.astype(BF16)
    return high, (values - high.astype(F32)).astype(BF16)


def dot_lanes(left, right):
    return lax.dot_general(left, right, (((1,), (1,)), ((), ())), preferred_element_type=F32)


def dot(left, right):
    return jnp.dot(left, right, preferred_element_type=F32)


def partner(block, axis, bit):
    count = lax.axis_size(axis)
    return lax.ppermute(block, axis, [(i, i ^ bit) for i in range(count)])


def shifted(block, axis, step):
    count = lax.axis_size(axis)
    return lax.ppermute(block, axis, [(i, i + step) for i in range(count) if 0 <= i + step < count])


class Pairs:
    def __init__(self, info, slots, atoms, face_rows, plane, me):
        def rows(first):
            return jnp.concatenate([ref[first * slots : (first + 1) * slots, :] for ref in info], axis=1)

        self.slots = slots
        self.harm, r2 = harmonics(rows(0), rows(1), rows(2))
        code = rows(3).astype(jnp.int32)
        tail = rows(4)
        slot = lax.broadcasted_iota(jnp.int32, code.shape, 0).astype(F32)
        active = (slot < tail[0:1, :]).astype(F32)
        self.target = tail[1:2, :]
        relative = (code & (plane - 1)) ^ me
        offset = code >> (plane.bit_length() - 1)
        width = jnp.where(offset < plane * atoms, atoms, 2 * face_rows)
        self.column = offset + relative * width
        envelope = (1.0 - r2 / 7.0) ** 2 * active
        self.basis_parts = (jnp.sqrt(r2), envelope)

    def radial(self, lhs_ref, out_ref, nbasis):
        distance, envelope = self.basis_parts
        values = [
            jnp.exp(-(((distance - SPACING * b) / SPACING) ** 2)) * envelope for b in range(nbasis)
        ]
        basis = jnp.concatenate(values, axis=0)
        high, low = split_high_low(basis)
        stack = jnp.concatenate([high, low, high], axis=0)
        out_ref[...] = dot(lhs_ref[...], stack)

    def table(self, k, total):
        column = self.column[k : k + 1, :]
        rows = lax.broadcasted_iota(jnp.int32, (total, column.shape[1]), 0)
        return jnp.where(rows == column, 1.0, 0.0).astype(BF16)

    def weight(self, lm, k):
        return self.harm[lm][k : k + 1, :]


def forward_kernel(slots, plane, me_ref, *refs):
    wide = refs[:plane]
    faces = refs[plane : 2 * plane]
    info = refs[2 * plane : 3 * plane]
    mix_ref, gate_ref, radial_ref, out_w_ref = refs[3 * plane : 3 * plane + 4]
    feats_ref, mixed_ref, gates_ref, msg_ref, dens_ref = refs[3 * plane + 4 : 3 * plane + 9]
    table_ref, coef_ref = refs[3 * plane + 9 :]
    atoms = wide[0].shape[1]
    edge = faces[0].shape[1]
    total = plane * (atoms + edge)
    part = mix_ref.shape[1] // 2
    for j in range(plane):
        feats_ref[:, j * atoms : (j + 1) * atoms, :] = wide[j][...]
        feats_ref[:, plane * atoms + j * edge : plane * atoms + (j + 1) * edge, :] = faces[j][...]
    gates_ref[...] = jax.nn.sigmoid(dot_lanes(gate_ref[...], feats_ref[0]))
    for lm in range(HARM):
        degree = DEGREE_OF[lm]
        both = dot_lanes(mix_ref[degree], feats_ref[lm])
        mixed, plain = both[:part], both[part:]
        mixed_ref[lm * part : (lm + 1) * part, :] = mixed
        if degree == 0:
            update = mixed * jax.nn.sigmoid(mixed)
        else:
            update = mixed * gates_ref[(degree - 1) * part : degree * part, :]
        table_ref[lm * part : (lm + 1) * part, :] = (plain + update).astype(BF16)
    pairs = Pairs(info, slots, atoms, edge // 2, plane, me_ref[0])
    nbasis = radial_ref.shape[1] // (3 * slots)
    pairs.radial(radial_ref, coef_ref, nbasis)
    message = jnp.zeros(msg_ref.shape, F32)
    for k in range(slots):
        rows = dot(table_ref[...], pairs.table(k, total))
        for degree, (start, end) in enumerate(DEGREE_SPANS):
            inner = None
            for lm in range(start, end):
                term = rows[lm * part : (lm + 1) * part]
                if lm > 0:
                    term = term * pairs.weight(lm, k)
                inner = term if inner is None else inner + term
            at = (k * 4 + degree) * part
            message = message + inner * coef_ref[at : at + part, :]
    msg_ref[...] = message
    partial = jnp.sum(message * jax.nn.sigmoid(message) * out_w_ref[...], axis=0, keepdims=True)
    dens_ref[...] = jnp.broadcast_to(partial, dens_ref.shape)


def backward_kernel(slots, plane, scale, probes_dev, me_ref, *refs):
    info = refs[:plane]
    dens = refs[plane : 2 * plane]
    feats_ref, mixed_ref, gates_ref, msg_ref, radial_ref, out_w_ref = refs[2 * plane : 2 * plane + 6]
    weight_ref, density_ref = refs[2 * plane + 6 : 2 * plane + 8]
    send_refs = refs[2 * plane + 8 : 3 * plane + 8]
    coef_ref, grad_ref = refs[3 * plane + 8 :]
    part = msg_ref.shape[0]
    total = feats_ref.shape[1]
    rows_out = send_refs[0].shape[0]
    atoms = 2 * rows_out // 3
    edge = rows_out - atoms
    probes = msg_ref.shape[1] // plane
    pairs = Pairs(info, slots, atoms, edge // 2, plane, me_ref[0])
    pairs.radial(radial_ref, coef_ref, radial_ref.shape[1] // (3 * slots))
    density = dens[0][0:1, :]
    for j in range(1, plane):
        other = dens[j][0:1, :]
        density = density + jnp.concatenate(
            [other[:, (b ^ j) * probes : ((b ^ j) + 1) * probes] for b in range(plane)], axis=1
        )
    density_ref[...] = jnp.broadcast_to(density[:, :probes], density_ref.shape)
    d_density = (density - pairs.target) * (1.0 / probes_dev)
    message = msg_ref[...]
    sig = jax.nn.sigmoid(message)
    d_message = d_density * out_w_ref[...] * (sig * (1.0 + message * (1.0 - sig)))
    for k in range(slots):
        pieces = []
        for degree, (start, end) in enumerate(DEGREE_SPANS):
            at = (k * 4 + degree) * part
            base = coef_ref[at : at + part, :] * d_message
            for lm in range(start, end):
                piece = base if lm == 0 else base * pairs.weight(lm, k)
                pieces.append(piece.astype(BF16))
        contribution = jnp.concatenate(pieces, axis=0)
        product = dot_lanes(contribution, pairs.table(k, total))
        if k == 0:
            grad_ref[...] = product
        else:
            grad_ref[...] += product
    for degree, (start, end) in enumerate(DEGREE_SPANS):
        sums = None
        gate_sum = None
        for lm in range(start, end):
            grad = grad_ref[lm * part : (lm + 1) * part, :]
            mixed = mixed_ref[lm * part : (lm + 1) * part, :]
            if degree == 0:
                s = jax.nn.sigmoid(mixed)
                d_mixed = grad * (s * (1.0 + mixed * (1.0 - s)))
            else:
                d_mixed = grad * gates_ref[(degree - 1) * part : degree * part, :]
                gate_sum = grad * mixed if gate_sum is None else gate_sum + grad * mixed
            high, low = split_high_low(d_mixed)
            product = dot(jnp.concatenate([high, low], axis=0), feats_ref[lm])
            sums = product if sums is None else sums + product
        weight_ref[degree * part : (degree + 1) * part, :] = (sums[:part] + sums[part:]) * scale
        if degree > 0:
            gates = gates_ref[(degree - 1) * part : degree * part, :]
            high, low = split_high_low(gate_sum * gates * (1.0 - gates))
            product = dot(jnp.concatenate([high, low], axis=0), feats_ref[0])
            at = (3 + degree) * part
            weight_ref[at : at + part, :] = (product[:part] + product[part:]) * scale
    turned = grad_ref[...].T
    for j in range(plane):
        send_refs[j][:atoms, :] = turned[j * atoms : (j + 1) * atoms].astype(BF16)
        at = plane * atoms + j * edge
        send_refs[j][atoms:, :] = turned[at : at + edge].astype(BF16)


def finish_kernel(plane, me_ref, *refs):
    slices = refs[:plane]
    below_ref, above_ref, feats_ref, mix_ref, gate_ref, out_ref = refs[plane:]
    atoms = feats_ref.shape[1]
    channels = feats_ref.shape[2]
    part = channels // plane
    face = below_ref.shape[1]
    per = channels // part
    me = me_ref[0]
    lane = lax.broadcasted_iota(jnp.int32, (atoms, channels), 1)
    gates = jax.nn.sigmoid(dot(feats_ref[0], gate_ref[...]))

    def slab(j, group):
        columns = slice(group * channels, (group + 1) * channels)
        own = slices[j][:atoms, columns].astype(F32)
        low = own[:face] + below_ref[j, :, columns].astype(F32)
        high = own[atoms - face :] + above_ref[j, :, columns].astype(F32)
        return jnp.concatenate([low, own[face : atoms - face], high], axis=0)

    upstream = []
    for group in range(HARM // per):
        blocks = [slab(j, group) for j in range(plane)]
        for place in range(per):
            total = None
            for j in range(plane):
                home = (me ^ j) * part
                shift = (home - place * part + channels) % channels
                moved = pltpu.roll(blocks[j], shift, 1)
                keep = jnp.where((lane >= home) & (lane < home + part), moved, 0.0)
                total = keep if total is None else total + keep
            upstream.append(total)
    gate_parts = []
    zero_row = None
    for degree, (start, end) in enumerate(DEGREE_SPANS):
        weight = mix_ref[degree]
        gate_sum = None
        for lm in range(start, end):
            mixed = dot(feats_ref[lm], weight)
            if degree == 0:
                s = jax.nn.sigmoid(mixed)
                d_mixed = upstream[lm] * (s * (1.0 + mixed * (1.0 - s)))
            else:
                d_mixed = upstream[lm] * gates[:, (degree - 1) * channels : degree * channels]
                product = upstream[lm] * mixed
                gate_sum = product if gate_sum is None else gate_sum + product
            high, low = split_high_low(d_mixed)
            back = dot_lanes(jnp.concatenate([high, low], axis=0), weight)
            result = upstream[lm] + back[:atoms] + back[atoms:]
            if degree == 0:
                zero_row = result
            else:
                out_ref[:, lm, :] = result
        if degree > 0:
            gate_parts.append(gate_sum)
    d_gate = jnp.concatenate(gate_parts, axis=1) * gates * (1.0 - gates)
    high, low = split_high_low(d_gate)
    back = dot_lanes(jnp.concatenate([high, low], axis=0), gate_ref[...])
    out_ref[:, 0, :] = zero_row + back[:atoms] + back[atoms:]


def assemble_kernel(plane, me_ref, *refs):
    pieces = refs[:plane]
    mix_ref, gate_ref = refs[plane : plane + 2]
    (joined_ref,) = refs[plane + 2 :]
    part = pieces[0].shape[0] // 7
    channels = plane * part
    for j in range(plane):
        home = pl.multiple_of((me_ref[0] ^ j) * part, part)
        for block in range(7):
            joined_ref[block, pl.ds(home, part), :] = pieces[j][block * part : (block + 1) * part, :]
    for block in range(4):
        mix_ref[block] = joined_ref[block].T
    for block in range(3):
        gate_ref[:, block * channels : (block + 1) * channels] = joined_ref[4 + block].T


def call(kernel, outs, scratch, scalars, *arrays):
    vmem = pl.BlockSpec(memory_space=pltpu.VMEM)
    return pl.pallas_call(
        kernel,
        out_shape=outs,
        in_specs=[pl.BlockSpec(memory_space=pltpu.SMEM)] + [vmem] * len(arrays),
        out_specs=jax.tree.map(lambda _: vmem, outs),
        scratch_shapes=scratch,
        compiler_params=pltpu.CompilerParams(vmem_limit_bytes=VMEM_BYTES),
    )(scalars, *arrays)


def body(
    atom_feats,
    mix_weight,
    gate_weight,
    radial_weight,
    out_weight,
    pair_vec,
    nbr_atom,
    nbr_count,
    target,
):
    atoms, harm_count, channels = atom_feats.shape
    slots, probes = nbr_atom.shape
    nbasis = radial_weight.shape[0]
    plane = lax.axis_size("xy")
    slabs = lax.axis_size("slab")
    part = channels // plane
    face = atoms // 4
    edge = 2 * face
    total = plane * (atoms + edge)
    lanes = plane * probes
    me = lax.axis_index("xy").astype(jnp.int32)
    me_arr = me[None]

    domain = nbr_atom // atoms
    row = nbr_atom % atoms
    step = domain // plane - lax.axis_index("slab")
    wide = plane * atoms
    offset = jnp.where(step == 0, row, jnp.where(step < 0, wide + row - (atoms - face), wide + face + row))
    code = offset * plane + domain % plane
    tail = jnp.concatenate(
        [nbr_count.astype(F32)[None], target[None], jnp.zeros((slots - 2, probes), F32)], axis=0
    )
    info = jnp.concatenate([pair_vec.reshape(3 * slots, probes), code.astype(F32), tail], axis=0)

    own = jnp.transpose(atom_feats, (1, 0, 2))
    from_below = shifted(own[:, atoms - face :, :], "slab", 1)
    from_above = shifted(own[:, :face, :], "slab", -1)
    faces = jnp.concatenate([from_below, from_above], axis=1)
    info, _ = lax.optimization_barrier((info, from_above))
    bits = [1 << b for b in reversed(range((plane - 1).bit_length()))]
    held = {0: (own, faces, info)}
    for bit in bits:
        for j in list(held):
            held[j ^ bit] = tuple(partner(x, "xy", bit) for x in held[j])
    pieces = [held[j] for j in range(plane)]

    first = me * part
    mix_part = lax.dynamic_slice_in_dim(mix_weight, first, part, axis=2)
    mix_part = jnp.transpose(mix_part, (0, 2, 1))
    pick = lax.broadcasted_iota(jnp.int32, (4, part, channels), 1) + first
    pick = (pick == lax.broadcasted_iota(jnp.int32, (4, part, channels), 2)).astype(BF16)
    mix_part = jnp.concatenate([mix_part, pick], axis=1)
    gate_part = lax.dynamic_slice_in_dim(gate_weight.reshape(channels, 3, channels), first, part, axis=2)
    gate_part = jnp.transpose(gate_part, (1, 2, 0)).reshape(3 * part, channels)
    radial_part = lax.dynamic_slice_in_dim(radial_weight.reshape(nbasis, 4, channels), first, part, axis=2)
    radial_part = jnp.transpose(radial_part, (1, 2, 0)).reshape(4 * part, nbasis)
    high = lax.reduce_precision(radial_part, 8, 7)
    three = jnp.stack([high, high, radial_part - high], axis=1)
    same = jnp.eye(slots, dtype=F32)
    radial_lhs = three[None, :, :, :, None] * same[:, None, None, None, :]
    radial_lhs = radial_lhs.reshape(slots * 4 * part, 3 * nbasis * slots).astype(BF16)
    out_part = lax.dynamic_slice_in_dim(out_weight, first, part)[:, None]

    infos = [p[2] for p in pieces]
    feats, mixed, gates, message, dens = call(
        functools.partial(forward_kernel, slots, plane),
        (
            jax.ShapeDtypeStruct((harm_count, total, channels), BF16),
            jax.ShapeDtypeStruct((harm_count * part, total), F32),
            jax.ShapeDtypeStruct((3 * part, total), F32),
            jax.ShapeDtypeStruct((part, lanes), F32),
            jax.ShapeDtypeStruct((8, lanes), F32),
        ),
        [
            pltpu.VMEM((harm_count * part, total), BF16),
            pltpu.VMEM((slots * 4 * part, lanes), F32),
        ],
        me_arr,
        *[p[0] for p in pieces],
        *[p[1] for p in pieces],
        *infos,
        mix_part,
        gate_part,
        radial_lhs,
        out_part,
    )
    dens_all = [dens] + [partner(dens, "xy", j) for j in range(1, plane)]

    outs = call(
        functools.partial(backward_kernel, slots, plane, 1.0 / float(slabs * plane), float(probes)),
        (
            jax.ShapeDtypeStruct((7 * part, channels), F32),
            jax.ShapeDtypeStruct((8, probes), F32),
        )
        + tuple(jax.ShapeDtypeStruct((atoms + edge, harm_count * part), BF16) for _ in range(plane)),
        [
            pltpu.VMEM((slots * 4 * part, lanes), F32),
            pltpu.VMEM((harm_count * part, total), F32),
        ],
        me_arr,
        *infos,
        *dens_all,
        feats,
        mixed,
        gates,
        message,
        radial_lhs,
        out_part,
    )
    weight, density, sends = outs[0], outs[1], list(outs[2:])

    steps = [1 << b for b in range((slabs - 1).bit_length())]
    weight = weight + partner(weight, "slab", steps[0])

    weight, *sends = lax.optimization_barrier((weight, *sends))
    slices = [sends[0]] + [partner(sends[j], "xy", j) for j in range(1, plane)]
    to_below = jnp.stack([s[atoms : atoms + face] for s in slices], axis=0)
    to_above = jnp.stack([s[atoms + face :] for s in slices], axis=0)
    grad_above = shifted(to_below, "slab", -1)
    grad_below = shifted(to_above, "slab", 1)
    feat_grad = call(
        functools.partial(finish_kernel, plane),
        jax.ShapeDtypeStruct((atoms, harm_count, channels), F32),
        [],
        me_arr,
        *slices,
        grad_below,
        grad_above,
        own,
        mix_weight,
        gate_weight,
    )

    for bit in steps[1:]:
        weight = weight + partner(weight, "slab", bit)
    columns = {0: weight}
    for bit in bits:
        for j in list(columns):
            columns[j ^ bit] = partner(columns[j], "xy", bit)
    mix_grad, gate_grad = call(
        functools.partial(assemble_kernel, plane),
        (
            jax.ShapeDtypeStruct((4, channels, channels), F32),
            jax.ShapeDtypeStruct((channels, 3 * channels), F32),
        ),
        [pltpu.VMEM((7, channels, channels), F32)],
        me_arr,
        *[columns[j] for j in range(plane)],
    )
    return (density[0], feat_grad, mix_grad, gate_grad)


def solution(mesh):
    in_specs = (
        P(("slab", "xy"), None, None),
        P(),
        P(),
        P(),
        P(),
        P(None, None, ("slab", "xy")),
        P(None, ("slab", "xy")),
        P(("slab", "xy")),
        P(("slab", "xy")),
    )
    out_specs = (P(("slab", "xy")), P(("slab", "xy"), None, None), P(), P())
    return jax.shard_map(body, mesh=mesh, in_specs=in_specs, out_specs=out_specs, check_vma=False)
```

```python
import functools
import math

import jax
import jax.numpy as jnp
from jax import lax
from jax.experimental import pallas as pl
from jax.experimental.pallas import tpu as pltpu
from jax.sharding import PartitionSpec as P

DEGREE_SPANS = ((0, 1), (1, 4), (4, 9), (9, 16))
DEGREE_OF = (0,) + (1,) * 3 + (2,) * 5 + (3,) * 7
HARM = 16
SPACING = 0.35
root_three = math.sqrt(3.0)
cubic_outer = math.sqrt(10.0) / 4.0
cubic_middle = math.sqrt(15.0)
cubic_inner = math.sqrt(6.0) / 4.0
VMEM_BYTES = 20 * 2**20
F32 = jnp.float32
BF16 = jnp.bfloat16
LAST_STEP = F32


def harmonics(x, y, z):
    r2 = x * x + y * y + z * z
    terms = [
        None,
        x,
        y,
        z,
        root_three * x * y,
        root_three * y * z,
        0.5 * (3.0 * z * z - r2),
        root_three * x * z,
        0.5 * root_three * (x * x - y * y),
        cubic_outer * y * (3.0 * x * x - y * y),
        cubic_middle * x * y * z,
        cubic_inner * y * (5.0 * z * z - r2),
        0.5 * z * (5.0 * z * z - 3.0 * r2),
        cubic_inner * x * (5.0 * z * z - r2),
        0.5 * cubic_middle * z * (x * x - y * y),
        cubic_outer * x * (x * x - 3.0 * y * y),
    ]
    return terms, r2


def split_high_low(values):
    high = values.astype(BF16)
    return high, (values - high.astype(F32)).astype(BF16)


def dot_lanes(left, right):
    return lax.dot_general(left, right, (((1,), (1,)), ((), ())), preferred_element_type=F32)


def dot(left, right):
    return jnp.dot(left, right, preferred_element_type=F32)


def partner(block, axis, bit):
    count = lax.axis_size(axis)
    return lax.ppermute(block, axis, [(i, i ^ bit) for i in range(count)])


def beside(block, axis, first):
    count = lax.axis_size(axis)
    start = 0 if first else 1
    pairs = [(i, i + 1) for i in range(start, count - 1, 2)]
    return lax.ppermute(block, axis, pairs + [(j, i) for i, j in pairs])


def table(column_ref, k, total):
    column = column_ref[k : k + 1, :]
    rows = lax.broadcasted_iota(jnp.int32, (total, column.shape[1]), 0)
    return jnp.where(rows == column, 1.0, 0.0).astype(BF16)


def geometry_kernel(slots, atoms, edge, plane, place_ref, *refs):
    info = refs[:plane]
    lhs_ref, coef_ref, harm_ref, column_ref, target_ref = refs[plane:]

    def rows(first):
        return jnp.concatenate([ref[first * slots : (first + 1) * slots, :] for ref in info], axis=1)

    harm, r2 = harmonics(rows(0), rows(1), rows(2))
    for lm in range(1, HARM):
        harm_ref[lm * slots : (lm + 1) * slots, :] = harm[lm]
    harm_ref[:slots, :] = jnp.ones_like(r2)
    code = rows(3).astype(jnp.int32)
    tail = rows(4)
    target_ref[...] = tail
    slot = lax.broadcasted_iota(jnp.int32, code.shape, 0).astype(F32)
    active = (slot < tail[0:1, :]).astype(F32)
    relative = (code & (plane - 1)) ^ (place_ref[0] >> 1)
    offset = code >> (plane.bit_length() - 1)
    column_ref[...] = offset + relative * jnp.where(offset < plane * atoms, atoms, edge)
    envelope = (1.0 - r2 / 7.0) ** 2 * active
    distance = jnp.sqrt(r2)
    nbasis = lhs_ref.shape[1] // (3 * slots)
    values = [jnp.exp(-(((distance - SPACING * b) / SPACING) ** 2)) * envelope for b in range(nbasis)]
    high, low = split_high_low(jnp.concatenate(values, axis=0))
    coef_ref[...] = dot(lhs_ref[...], jnp.concatenate([high, low, high], axis=0))


def forward_kernel(slots, plane, *refs):
    wide = refs[:plane]
    faces = refs[plane : 2 * plane]
    coef_ref, harm_ref, column_ref, mix_ref, gate_ref, out_w_ref = refs[2 * plane : 2 * plane + 6]
    feats_ref, mixed_ref, gates_ref, msg_ref, dens_ref, source_ref = refs[2 * plane + 6 :]
    atoms = wide[0].shape[1]
    edge = faces[0].shape[1]
    total = plane * (atoms + edge)
    part = mix_ref.shape[1] // 2
    for j in range(plane):
        feats_ref[:, j * atoms : (j + 1) * atoms, :] = wide[j][...]
        feats_ref[:, plane * atoms + j * edge : plane * atoms + (j + 1) * edge, :] = faces[j][...]
    gates_ref[...] = jax.nn.sigmoid(dot_lanes(gate_ref[...], feats_ref[0]))
    for lm in range(HARM):
        degree = DEGREE_OF[lm]
        both = dot_lanes(mix_ref[degree], feats_ref[lm])
        mixed, plain = both[:part], both[part:]
        mixed_ref[lm * part : (lm + 1) * part, :] = mixed
        if degree == 0:
            update = mixed * jax.nn.sigmoid(mixed)
        else:
            update = mixed * gates_ref[(degree - 1) * part : degree * part, :]
        source_ref[lm * part : (lm + 1) * part, :] = (plain + update).astype(BF16)
    message = jnp.zeros(msg_ref.shape, F32)
    for k in range(slots):
        rows = dot(source_ref[...], table(column_ref, k, total))
        for degree, (start, end) in enumerate(DEGREE_SPANS):
            inner = None
            for lm in range(start, end):
                term = rows[lm * part : (lm + 1) * part]
                if lm > 0:
                    term = term * harm_ref[lm * slots + k : lm * slots + k + 1, :]
                inner = term if inner is None else inner + term
            at = (k * 4 + degree) * part
            message = message + inner * coef_ref[at : at + part, :]
    msg_ref[...] = message
    partial = jnp.sum(message * jax.nn.sigmoid(message) * out_w_ref[...], axis=0, keepdims=True)
    dens_ref[...] = jnp.broadcast_to(partial, dens_ref.shape)


def backward_kernel(slots, plane, scale, probes_dev, *refs):
    dens = refs[:plane]
    coef_ref, harm_ref, column_ref, target_ref, feats_ref = refs[plane : plane + 5]
    mixed_ref, gates_ref, msg_ref, out_w_ref = refs[plane + 5 : plane + 9]
    weight_ref, density_ref = refs[plane + 9 : plane + 11]
    send_refs = refs[plane + 11 : -1]
    grad_ref = refs[-1]
    part = msg_ref.shape[0]
    total = feats_ref.shape[1]
    rows_out = send_refs[0].shape[0]
    atoms = 2 * rows_out // 3
    edge = rows_out - atoms
    probes = msg_ref.shape[1] // plane
    density = dens[0][0:1, :]
    for j in range(1, plane):
        other = dens[j][0:1, :]
        density = density + jnp.concatenate(
            [other[:, (b ^ j) * probes : ((b ^ j) + 1) * probes] for b in range(plane)], axis=1
        )
    density_ref[...] = jnp.broadcast_to(density[:, :probes], density_ref.shape)
    d_density = (density - target_ref[1:2, :]) * (1.0 / probes_dev)
    message = msg_ref[...]
    sig = jax.nn.sigmoid(message)
    d_message = d_density * out_w_ref[...] * (sig * (1.0 + message * (1.0 - sig)))
    for k in range(slots):
        pieces = []
        for degree, (start, end) in enumerate(DEGREE_SPANS):
            at = (k * 4 + degree) * part
            base = coef_ref[at : at + part, :] * d_message
            for lm in range(start, end):
                piece = base if lm == 0 else base * harm_ref[lm * slots + k : lm * slots + k + 1, :]
                pieces.append(piece.astype(BF16))
        contribution = jnp.concatenate(pieces, axis=0)
        product = dot_lanes(contribution, table(column_ref, k, total))
        if k == 0:
            grad_ref[...] = product
        else:
            grad_ref[...] += product
    for degree, (start, end) in enumerate(DEGREE_SPANS):
        sums = None
        gate_sum = None
        for lm in range(start, end):
            grad = grad_ref[lm * part : (lm + 1) * part, :]
            mixed = mixed_ref[lm * part : (lm + 1) * part, :]
            if degree == 0:
                s = jax.nn.sigmoid(mixed)
                d_mixed = grad * (s * (1.0 + mixed * (1.0 - s)))
            else:
                d_mixed = grad * gates_ref[(degree - 1) * part : degree * part, :]
                gate_sum = grad * mixed if gate_sum is None else gate_sum + grad * mixed
            high, low = split_high_low(d_mixed)
            product = dot(jnp.concatenate([high, low], axis=0), feats_ref[lm])
            sums = product if sums is None else sums + product
        weight_ref[degree * part : (degree + 1) * part, :] = (sums[:part] + sums[part:]) * scale
        if degree > 0:
            gates = gates_ref[(degree - 1) * part : degree * part, :]
            high, low = split_high_low(gate_sum * gates * (1.0 - gates))
            product = dot(jnp.concatenate([high, low], axis=0), feats_ref[0])
            at = (3 + degree) * part
            weight_ref[at : at + part, :] = (product[:part] + product[part:]) * scale
    turned = grad_ref[...].T
    for j in range(plane):
        send_ref = send_refs[j.bit_length()]
        first = (j - (1 << j.bit_length() >> 1)) * rows_out
        send_ref[first : first + atoms, :] = turned[j * atoms : (j + 1) * atoms].astype(BF16)
        at = plane * atoms + j * edge
        send_ref[first + atoms : first + rows_out, :] = turned[at : at + edge].astype(BF16)


def finish_kernel(plane, firsts, place_ref, *refs):
    slices = refs[:plane]
    near_ref, far_ref, feats_ref, mix_ref, gate_ref, out_ref = refs[plane:]
    atoms = feats_ref.shape[1]
    channels = feats_ref.shape[2]
    part = channels // plane
    face = near_ref.shape[1]
    odd = (jnp.zeros((face, channels), jnp.int32) + place_ref[0]) % 2 > 0
    per = channels // part
    me = place_ref[0] >> 1
    lane = lax.broadcasted_iota(jnp.int32, (atoms, channels), 1)
    gates = jax.nn.sigmoid(dot(feats_ref[0], gate_ref[...]))

    def slab(j, group):
        columns = slice(group * channels, (group + 1) * channels)
        own = slices[j][firsts[j] : firsts[j] + atoms, columns].astype(F32)
        near, far = near_ref[j, :, columns].astype(F32), far_ref[j, :, columns].astype(F32)
        low = own[:face] + jnp.where(odd, near, far)
        high = own[atoms - face :] + jnp.where(odd, far, near)
        return jnp.concatenate([low, own[face : atoms - face], high], axis=0)

    upstream = []
    for group in range(HARM // per):
        blocks = [slab(j, group) for j in range(plane)]
        for place in range(per):
            total = None
            for j in range(plane):
                home = (me ^ j) * part
                shift = (home - place * part + channels) % channels
                moved = pltpu.roll(blocks[j], shift, 1)
                keep = jnp.where((lane >= home) & (lane < home + part), moved, 0.0)
                total = keep if total is None else total + keep
            upstream.append(total)
    gate_parts = []
    zero_row = None
    for degree, (start, end) in enumerate(DEGREE_SPANS):
        weight = mix_ref[degree]
        gate_sum = None
        for lm in range(start, end):
            mixed = dot(feats_ref[lm], weight)
            if degree == 0:
                s = jax.nn.sigmoid(mixed)
                d_mixed = upstream[lm] * (s * (1.0 + mixed * (1.0 - s)))
            else:
                d_mixed = upstream[lm] * gates[:, (degree - 1) * channels : degree * channels]
                product = upstream[lm] * mixed
                gate_sum = product if gate_sum is None else gate_sum + product
            high, low = split_high_low(d_mixed)
            back = dot_lanes(jnp.concatenate([high, low], axis=0), weight)
            result = upstream[lm] + back[:atoms] + back[atoms:]
            if degree == 0:
                zero_row = result
            else:
                out_ref[:, lm, :] = result
        if degree > 0:
            gate_parts.append(gate_sum)
    d_gate = jnp.concatenate(gate_parts, axis=1) * gates * (1.0 - gates)
    high, low = split_high_low(d_gate)
    back = dot_lanes(jnp.concatenate([high, low], axis=0), gate_ref[...])
    out_ref[:, 0, :] = zero_row + back[:atoms] + back[atoms:]


def assemble_kernel(plane, place_ref, *refs):
    pieces = refs[:plane]
    mix_ref, gate_ref = refs[plane : plane + 2]
    (joined_ref,) = refs[plane + 2 :]
    part = pieces[0].shape[0] // 7
    channels = plane * part
    for j in range(plane):
        home = pl.multiple_of(((place_ref[0] >> 1) ^ j) * part, part)
        for block in range(7):
            joined_ref[block, pl.ds(home, part), :] = pieces[j][block * part : (block + 1) * part, :]
    for block in range(4):
        mix_ref[block] = joined_ref[block].T
    for block in range(3):
        gate_ref[:, block * channels : (block + 1) * channels] = joined_ref[4 + block].T


def call(kernel, outs, scratch, *arrays):
    vmem = pl.BlockSpec(memory_space=pltpu.VMEM)
    smem = pl.BlockSpec(memory_space=pltpu.SMEM)
    return pl.pallas_call(
        kernel,
        out_shape=outs,
        in_specs=[smem if x.shape == (1,) else vmem for x in arrays],
        out_specs=jax.tree.map(lambda _: vmem, outs),
        scratch_shapes=scratch,
        compiler_params=pltpu.CompilerParams(vmem_limit_bytes=VMEM_BYTES),
    )(*arrays)


def body(
    atom_feats,
    mix_weight,
    gate_weight,
    radial_weight,
    out_weight,
    pair_vec,
    nbr_atom,
    nbr_count,
    target,
):
    atoms, harm_count, channels = atom_feats.shape
    slots, probes = nbr_atom.shape
    nbasis = radial_weight.shape[0]
    plane = lax.axis_size("xy")
    slabs = lax.axis_size("slab")
    part = channels // plane
    face = atoms // 4
    edge = 2 * face
    total = plane * (atoms + edge)
    lanes = plane * probes
    me = lax.axis_index("xy").astype(jnp.int32)
    slab = lax.axis_index("slab").astype(jnp.int32)
    odd = slab % 2
    place = (me * 2 + odd)[None]

    domain = nbr_atom // atoms
    row = nbr_atom % atoms
    step = domain // plane - slab
    wide = plane * atoms
    below = wide + (1 - odd) * face + row - (atoms - face)
    above = wide + odd * face + row
    offset = jnp.where(step == 0, row, jnp.where(step < 0, below, above))
    code = offset * plane + domain % plane
    tail = jnp.concatenate(
        [nbr_count.astype(F32)[None], target[None], jnp.zeros((slots - 2, probes), F32)], axis=0
    )
    info = jnp.concatenate([pair_vec.reshape(3 * slots, probes), code.astype(F32), tail], axis=0)

    own = jnp.transpose(atom_feats, (1, 0, 2))
    last = atoms - face
    near = beside(lax.dynamic_slice_in_dim(own, (1 - odd) * last, face, 1), "slab", True)
    far = beside(lax.dynamic_slice_in_dim(own, odd * last, face, 1), "slab", False)
    faces = jnp.concatenate([near, far], axis=1)
    info, near = lax.optimization_barrier((info, near))
    bits = [1 << b for b in reversed(range((plane - 1).bit_length()))]
    infos = [info] + [partner(info, "xy", j) for j in range(1, plane)]
    held = {0: (own, faces)}
    for bit in bits:
        for j in list(held):
            held[j ^ bit] = tuple(partner(x, "xy", bit) for x in held[j])
    pieces = [held[j] for j in range(plane)]

    first = me * part
    mix_part = lax.dynamic_slice_in_dim(mix_weight, first, part, axis=2)
    mix_part = jnp.transpose(mix_part, (0, 2, 1))
    pick = lax.broadcasted_iota(jnp.int32, (4, part, channels), 1) + first
    pick = (pick == lax.broadcasted_iota(jnp.int32, (4, part, channels), 2)).astype(BF16)
    mix_part = jnp.concatenate([mix_part, pick], axis=1)
    gate_part = lax.dynamic_slice_in_dim(gate_weight.reshape(channels, 3, channels), first, part, axis=2)
    gate_part = jnp.transpose(gate_part, (1, 2, 0)).reshape(3 * part, channels)
    radial_part = lax.dynamic_slice_in_dim(radial_weight.reshape(nbasis, 4, channels), first, part, axis=2)
    radial_part = jnp.transpose(radial_part, (1, 2, 0)).reshape(4 * part, nbasis)
    high = lax.reduce_precision(radial_part, 8, 7)
    three = jnp.stack([high, high, radial_part - high], axis=1)
    same = jnp.eye(slots, dtype=F32)
    radial_lhs = three[None, :, :, :, None] * same[:, None, None, None, :]
    radial_lhs = radial_lhs.reshape(slots * 4 * part, 3 * nbasis * slots).astype(BF16)
    out_part = lax.dynamic_slice_in_dim(out_weight, first, part)[:, None]

    coef, harm, column, goals = call(
        functools.partial(geometry_kernel, slots, atoms, edge, plane),
        (
            jax.ShapeDtypeStruct((slots * 4 * part, lanes), F32),
            jax.ShapeDtypeStruct((harm_count * slots, lanes), F32),
            jax.ShapeDtypeStruct((slots, lanes), jnp.int32),
            jax.ShapeDtypeStruct((slots, lanes), F32),
        ),
        [],
        place,
        *infos,
        radial_lhs,
    )
    feats, mixed, gates, message, dens = call(
        functools.partial(forward_kernel, slots, plane),
        (
            jax.ShapeDtypeStruct((harm_count, total, channels), BF16),
            jax.ShapeDtypeStruct((harm_count * part, total), F32),
            jax.ShapeDtypeStruct((3 * part, total), F32),
            jax.ShapeDtypeStruct((part, lanes), F32),
            jax.ShapeDtypeStruct((8, lanes), F32),
        ),
        [pltpu.VMEM((harm_count * part, total), BF16)],
        *[p[0] for p in pieces],
        *[p[1] for p in pieces],
        coef,
        harm,
        column,
        mix_part,
        gate_part,
        out_part,
    )
    dens_all = [dens] + [partner(dens, "xy", j) for j in range(1, plane)]

    groups = [1] + [1 << b for b in range((plane - 1).bit_length())]
    outs = call(
        functools.partial(backward_kernel, slots, plane, 1.0 / float(slabs * plane), float(probes)),
        (
            jax.ShapeDtypeStruct((7 * part, channels), F32),
            jax.ShapeDtypeStruct((8, probes), F32),
        )
        + tuple(jax.ShapeDtypeStruct((rows * (atoms + edge), harm_count * part), BF16) for rows in groups),
        [pltpu.VMEM((harm_count * part, total), F32)],
        *dens_all,
        coef,
        harm,
        column,
        goals,
        feats,
        mixed,
        gates,
        message,
        out_part,
    )
    weight, density, sends = outs[0], outs[1], list(outs[2:])

    steps = [1 << b for b in range((slabs - 1).bit_length())]
    size = atoms + edge
    entries = [(0, sends[0], {0: 0})]
    for b, block in enumerate(sends[1:]):
        entries.append((0, block, {j: (j - (1 << b)) * size for j in range(1 << b, 2 << b)}))
    for bit in bits:
        due = [e for e in entries if any(bit <= j < 2 * bit for j in e[2])]
        for source, block, places in due:
            moved = {j ^ bit: at for j, at in places.items()}
            entries.append((source ^ bit, partner(block, "xy", bit), moved))
    mine = {source: (block, places[0]) for source, block, places in entries if 0 in places}
    slices = [mine[j][0] for j in range(plane)]
    firsts = tuple(mine[j][1] for j in range(plane))
    for bit in steps[:-1]:
        weight = weight + partner(weight, "slab", bit)
    weight = weight.astype(LAST_STEP)
    weight, *slices = lax.optimization_barrier((weight, *slices))
    weight = (weight, partner(weight, "slab", steps[-1]))
    edges = [s[f + atoms : f + size] for s, f in zip(slices, firsts)]
    near_grad = beside(jnp.stack([e[:face] for e in edges], axis=0), "slab", True)
    far_grad = beside(jnp.stack([e[face:] for e in edges], axis=0), "slab", False)
    *weight, near_grad, far_grad = lax.optimization_barrier((*weight, near_grad, far_grad))
    weight = weight[0].astype(F32) + weight[1].astype(F32)
    feat_grad = call(
        functools.partial(finish_kernel, plane, firsts),
        jax.ShapeDtypeStruct((atoms, harm_count, channels), F32),
        [],
        place,
        *slices,
        near_grad,
        far_grad,
        own,
        mix_weight,
        gate_weight,
    )

    columns = {0: weight}
    for bit in bits:
        arrived = {j ^ bit: partner(columns[j], "xy", bit) for j in columns}
        if bit == bits[0]:
            *values, feat_grad = lax.optimization_barrier((*arrived.values(), feat_grad))
            arrived = dict(zip(arrived, values))
        columns.update(arrived)
    mix_grad, gate_grad = call(
        functools.partial(assemble_kernel, plane),
        (
            jax.ShapeDtypeStruct((4, channels, channels), F32),
            jax.ShapeDtypeStruct((channels, 3 * channels), F32),
        ),
        [pltpu.VMEM((7, channels, channels), F32)],
        place,
        *[columns[j] for j in range(plane)],
    )
    return (density[0], feat_grad, mix_grad, gate_grad)


def solution(mesh):
    in_specs = (
        P(("slab", "xy"), None, None),
        P(),
        P(),
        P(),
        P(),
        P(None, None, ("slab", "xy")),
        P(None, ("slab", "xy")),
        P(("slab", "xy")),
        P(("slab", "xy")),
    )
    out_specs = (P(("slab", "xy")), P(("slab", "xy"), None, None), P(), P())
    return jax.shard_map(body, mesh=mesh, in_specs=in_specs, out_specs=out_specs, check_vma=False)
```

```python
import functools
import math

import jax
import jax.numpy as jnp
from jax import lax
from jax.experimental import pallas as pl
from jax.experimental.pallas import tpu as pltpu
from jax.sharding import PartitionSpec as P

DEGREE_SPANS = ((0, 1), (1, 4), (4, 9), (9, 16))
DEGREE_OF = (0,) + (1,) * 3 + (2,) * 5 + (3,) * 7
HARM = 16
SPACING = 0.35
root_three = math.sqrt(3.0)
cubic_outer = math.sqrt(10.0) / 4.0
cubic_middle = math.sqrt(15.0)
cubic_inner = math.sqrt(6.0) / 4.0
VMEM_BYTES = 20 * 2**20
F32 = jnp.float32
BF16 = jnp.bfloat16
LAST_STEP = BF16


def harmonics(x, y, z):
    r2 = x * x + y * y + z * z
    terms = [
        None,
        x,
        y,
        z,
        root_three * x * y,
        root_three * y * z,
        0.5 * (3.0 * z * z - r2),
        root_three * x * z,
        0.5 * root_three * (x * x - y * y),
        cubic_outer * y * (3.0 * x * x - y * y),
        cubic_middle * x * y * z,
        cubic_inner * y * (5.0 * z * z - r2),
        0.5 * z * (5.0 * z * z - 3.0 * r2),
        cubic_inner * x * (5.0 * z * z - r2),
        0.5 * cubic_middle * z * (x * x - y * y),
        cubic_outer * x * (x * x - 3.0 * y * y),
    ]
    return terms, r2


def split_high_low(values):
    high = values.astype(BF16)
    return high, (values - high.astype(F32)).astype(BF16)


def dot_lanes(left, right):
    return lax.dot_general(left, right, (((1,), (1,)), ((), ())), preferred_element_type=F32)


def dot(left, right):
    return jnp.dot(left, right, preferred_element_type=F32)


def partner(block, axis, bit):
    count = lax.axis_size(axis)
    return lax.ppermute(block, axis, [(i, i ^ bit) for i in range(count)])


def beside(block, axis, first):
    count = lax.axis_size(axis)
    pairs = [(i, (i + 1) % count) for i in range(0 if first else 1, count, 2)]
    return lax.ppermute(block, axis, pairs + [(j, i) for i, j in pairs])


def table(column_ref, k, total):
    column = column_ref[k : k + 1, :]
    rows = lax.broadcasted_iota(jnp.int32, (total, column.shape[1]), 0)
    return jnp.where(rows == column, 1.0, 0.0).astype(BF16)


def geometry_kernel(slots, atoms, edge, plane, place_ref, *refs):
    rows_of = (refs[0].shape[0] - HARM * edge) // 3
    info = [
        sum(ref[HARM * edge + i * rows_of : HARM * edge + (i + 1) * rows_of, :].astype(F32) for i in range(3))
        for ref in refs[:plane]
    ]
    lhs_ref, coef_ref, harm_ref, column_ref, target_ref = refs[plane:]

    def rows(first):
        return jnp.concatenate([x[first * slots : (first + 1) * slots, :] for x in info], axis=1)

    harm, r2 = harmonics(rows(0), rows(1), rows(2))
    for lm in range(1, HARM):
        harm_ref[lm * slots : (lm + 1) * slots, :] = harm[lm]
    harm_ref[:slots, :] = jnp.ones_like(r2)
    code = rows(3).astype(jnp.int32)
    tail = rows(4)
    target_ref[...] = tail
    slot = lax.broadcasted_iota(jnp.int32, code.shape, 0).astype(F32)
    active = (slot < tail[0:1, :]).astype(F32)
    relative = (code & (plane - 1)) ^ (place_ref[0] >> 1)
    offset = code >> (plane.bit_length() - 1)
    column_ref[...] = offset + relative * jnp.where(offset < plane * atoms, atoms, edge)
    envelope = (1.0 - r2 / 7.0) ** 2 * active
    distance = jnp.sqrt(r2)
    nbasis = lhs_ref.shape[1] // (3 * slots)
    values = [jnp.exp(-(((distance - SPACING * b) / SPACING) ** 2)) * envelope for b in range(nbasis)]
    high, low = split_high_low(jnp.concatenate(values, axis=0))
    coef_ref[...] = dot(lhs_ref[...], jnp.concatenate([high, low, high], axis=0))


def forward_kernel(slots, plane, *refs):
    wide = refs[:plane]
    faces = refs[plane : 2 * plane]
    coef_ref, harm_ref, column_ref, mix_ref, gate_ref, out_w_ref = refs[2 * plane : 2 * plane + 6]
    feats_ref, mixed_ref, gates_ref, msg_ref, dens_ref, source_ref = refs[2 * plane + 6 :]
    atoms = wide[0].shape[1]
    edge = (feats_ref.shape[1] - plane * atoms) // plane
    face = edge // 2
    total = plane * (atoms + edge)
    part = mix_ref.shape[1] // 2
    for j in range(plane):
        feats_ref[:, j * atoms : (j + 1) * atoms, :] = wide[j][...]
        for side in range(2):
            at = plane * atoms + j * edge + side * face
            for lm in range(HARM):
                first = (side * HARM + lm) * face
                feats_ref[lm, at : at + face, :] = faces[j][first : first + face, :]
    gates_ref[...] = jax.nn.sigmoid(dot_lanes(gate_ref[...], feats_ref[0]))
    for lm in range(HARM):
        degree = DEGREE_OF[lm]
        both = dot_lanes(mix_ref[degree], feats_ref[lm])
        mixed, plain = both[:part], both[part:]
        mixed_ref[lm * part : (lm + 1) * part, :] = mixed
        if degree == 0:
            update = mixed * jax.nn.sigmoid(mixed)
        else:
            update = mixed * gates_ref[(degree - 1) * part : degree * part, :]
        source_ref[lm * part : (lm + 1) * part, :] = (plain + update).astype(BF16)
    message = jnp.zeros(msg_ref.shape, F32)
    for k in range(slots):
        rows = dot(source_ref[...], table(column_ref, k, total))
        for degree, (start, end) in enumerate(DEGREE_SPANS):
            inner = None
            for lm in range(start, end):
                term = rows[lm * part : (lm + 1) * part]
                if lm > 0:
                    term = term * harm_ref[lm * slots + k : lm * slots + k + 1, :]
                inner = term if inner is None else inner + term
            at = (k * 4 + degree) * part
            message = message + inner * coef_ref[at : at + part, :]
    msg_ref[...] = message
    partial = jnp.sum(message * jax.nn.sigmoid(message) * out_w_ref[...], axis=0, keepdims=True)
    dens_ref[...] = jnp.broadcast_to(partial, dens_ref.shape)


def backward_kernel(slots, plane, scale, probes_dev, *refs):
    dens = refs[:plane]
    coef_ref, harm_ref, column_ref, target_ref, feats_ref = refs[plane : plane + 5]
    mixed_ref, gates_ref, msg_ref, out_w_ref = refs[plane + 5 : plane + 9]
    weight_ref, density_ref = refs[plane + 9 : plane + 11]
    send_refs = refs[plane + 11 : -1]
    grad_ref = refs[-1]
    part = msg_ref.shape[0]
    total = feats_ref.shape[1]
    rows_out = send_refs[0].shape[0]
    atoms = 2 * rows_out // 3
    edge = rows_out - atoms
    probes = msg_ref.shape[1] // plane
    density = dens[0][0:1, :]
    for j in range(1, plane):
        other = dens[j][0:1, :]
        density = density + jnp.concatenate(
            [other[:, (b ^ j) * probes : ((b ^ j) + 1) * probes] for b in range(plane)], axis=1
        )
    density_ref[...] = jnp.broadcast_to(density[:, :probes], density_ref.shape)
    d_density = (density - target_ref[1:2, :]) * (1.0 / probes_dev)
    message = msg_ref[...]
    sig = jax.nn.sigmoid(message)
    d_message = d_density * out_w_ref[...] * (sig * (1.0 + message * (1.0 - sig)))
    for k in range(slots):
        pieces = []
        for degree, (start, end) in enumerate(DEGREE_SPANS):
            at = (k * 4 + degree) * part
            base = coef_ref[at : at + part, :] * d_message
            for lm in range(start, end):
                piece = base if lm == 0 else base * harm_ref[lm * slots + k : lm * slots + k + 1, :]
                pieces.append(piece.astype(BF16))
        contribution = jnp.concatenate(pieces, axis=0)
        product = dot_lanes(contribution, table(column_ref, k, total))
        if k == 0:
            grad_ref[...] = product
        else:
            grad_ref[...] += product
    for degree, (start, end) in enumerate(DEGREE_SPANS):
        sums = None
        gate_sum = None
        for lm in range(start, end):
            grad = grad_ref[lm * part : (lm + 1) * part, :]
            mixed = mixed_ref[lm * part : (lm + 1) * part, :]
            if degree == 0:
                s = jax.nn.sigmoid(mixed)
                d_mixed = grad * (s * (1.0 + mixed * (1.0 - s)))
            else:
                d_mixed = grad * gates_ref[(degree - 1) * part : degree * part, :]
                gate_sum = grad * mixed if gate_sum is None else gate_sum + grad * mixed
            high, low = split_high_low(d_mixed)
            product = dot(jnp.concatenate([high, low], axis=0), feats_ref[lm])
            sums = product if sums is None else sums + product
        weight_ref[degree * part : (degree + 1) * part, :] = (sums[:part] + sums[part:]) * scale
        if degree > 0:
            gates = gates_ref[(degree - 1) * part : degree * part, :]
            high, low = split_high_low(gate_sum * gates * (1.0 - gates))
            product = dot(jnp.concatenate([high, low], axis=0), feats_ref[0])
            at = (3 + degree) * part
            weight_ref[at : at + part, :] = (product[:part] + product[part:]) * scale
    turned = grad_ref[...].T
    for j in range(plane):
        send_ref = send_refs[j.bit_length()]
        first = (j - (1 << j.bit_length() >> 1)) * rows_out
        send_ref[first : first + atoms, :] = turned[j * atoms : (j + 1) * atoms].astype(BF16)
        at = plane * atoms + j * edge
        send_ref[first + atoms : first + rows_out, :] = turned[at : at + edge].astype(BF16)


def finish_kernel(plane, firsts, place_ref, *refs):
    slices = refs[:plane]
    near_ref, far_ref, feats_ref, mix_ref, gate_ref, out_ref = refs[plane:]
    atoms = feats_ref.shape[1]
    channels = feats_ref.shape[2]
    part = channels // plane
    face = near_ref.shape[1]
    odd = (jnp.zeros((face, channels), jnp.int32) + place_ref[0]) % 2 > 0
    per = channels // part
    me = place_ref[0] >> 1
    lane = lax.broadcasted_iota(jnp.int32, (atoms, channels), 1)
    gates = jax.nn.sigmoid(dot(feats_ref[0], gate_ref[...]))

    def slab(j, group):
        columns = slice(group * channels, (group + 1) * channels)
        own = slices[j][firsts[j] : firsts[j] + atoms, columns].astype(F32)
        near, far = near_ref[j, :, columns].astype(F32), far_ref[j, :, columns].astype(F32)
        low = own[:face] + jnp.where(odd, near, far)
        high = own[atoms - face :] + jnp.where(odd, far, near)
        return jnp.concatenate([low, own[face : atoms - face], high], axis=0)

    upstream = []
    for group in range(HARM // per):
        blocks = [slab(j, group) for j in range(plane)]
        for place in range(per):
            total = None
            for j in range(plane):
                home = (me ^ j) * part
                shift = (home - place * part + channels) % channels
                moved = pltpu.roll(blocks[j], shift, 1)
                keep = jnp.where((lane >= home) & (lane < home + part), moved, 0.0)
                total = keep if total is None else total + keep
            upstream.append(total)
    gate_parts = []
    zero_row = None
    for degree, (start, end) in enumerate(DEGREE_SPANS):
        weight = mix_ref[degree]
        gate_sum = None
        for lm in range(start, end):
            mixed = dot(feats_ref[lm], weight)
            if degree == 0:
                s = jax.nn.sigmoid(mixed)
                d_mixed = upstream[lm] * (s * (1.0 + mixed * (1.0 - s)))
            else:
                d_mixed = upstream[lm] * gates[:, (degree - 1) * channels : degree * channels]
                product = upstream[lm] * mixed
                gate_sum = product if gate_sum is None else gate_sum + product
            high, low = split_high_low(d_mixed)
            back = dot_lanes(jnp.concatenate([high, low], axis=0), weight)
            result = upstream[lm] + back[:atoms] + back[atoms:]
            if degree == 0:
                zero_row = result
            else:
                out_ref[:, lm, :] = result
        if degree > 0:
            gate_parts.append(gate_sum)
    d_gate = jnp.concatenate(gate_parts, axis=1) * gates * (1.0 - gates)
    high, low = split_high_low(d_gate)
    back = dot_lanes(jnp.concatenate([high, low], axis=0), gate_ref[...])
    out_ref[:, 0, :] = zero_row + back[:atoms] + back[atoms:]


def assemble_kernel(plane, place_ref, *refs):
    pieces = refs[:plane]
    mix_ref, gate_ref = refs[plane : plane + 2]
    (joined_ref,) = refs[plane + 2 :]
    part = pieces[0].shape[0] // 7
    channels = plane * part
    for j in range(plane):
        home = pl.multiple_of(((place_ref[0] >> 1) ^ j) * part, part)
        for block in range(7):
            joined_ref[block, pl.ds(home, part), :] = pieces[j][block * part : (block + 1) * part, :]
    for block in range(4):
        mix_ref[block] = joined_ref[block].T
    for block in range(3):
        gate_ref[:, block * channels : (block + 1) * channels] = joined_ref[4 + block].T


def call(kernel, outs, scratch, *arrays):
    vmem = pl.BlockSpec(memory_space=pltpu.VMEM)
    smem = pl.BlockSpec(memory_space=pltpu.SMEM)
    return pl.pallas_call(
        kernel,
        out_shape=outs,
        in_specs=[smem if x.shape == (1,) else vmem for x in arrays],
        out_specs=jax.tree.map(lambda _: vmem, outs),
        scratch_shapes=scratch,
        compiler_params=pltpu.CompilerParams(vmem_limit_bytes=VMEM_BYTES),
    )(*arrays)


def body(
    atom_feats,
    mix_weight,
    gate_weight,
    radial_weight,
    out_weight,
    pair_vec,
    nbr_atom,
    nbr_count,
    target,
):
    atoms, harm_count, channels = atom_feats.shape
    slots, probes = nbr_atom.shape
    nbasis = radial_weight.shape[0]
    plane = lax.axis_size("xy")
    slabs = lax.axis_size("slab")
    part = channels // plane
    face = atoms // 4
    edge = 2 * face
    total = plane * (atoms + edge)
    lanes = plane * probes
    me = lax.axis_index("xy").astype(jnp.int32)
    slab = lax.axis_index("slab").astype(jnp.int32)
    odd = slab % 2
    place = (me * 2 + odd)[None]

    domain = nbr_atom // atoms
    row = nbr_atom % atoms
    step = domain // plane - slab
    wide = plane * atoms
    below = wide + (1 - odd) * face + row - (atoms - face)
    above = wide + odd * face + row
    offset = jnp.where(step == 0, row, jnp.where(step < 0, below, above))
    code = offset * plane + domain % plane
    tail = jnp.concatenate(
        [nbr_count.astype(F32)[None], target[None], jnp.zeros((2 * slots - 2, probes), F32)], axis=0
    )
    info = jnp.concatenate([pair_vec.reshape(3 * slots, probes), code.astype(F32), tail], axis=0)

    own = jnp.transpose(atom_feats, (1, 0, 2))
    last = atoms - face
    near = beside(lax.dynamic_slice_in_dim(own, (1 - odd) * last, face, 1), "slab", True)
    far = beside(lax.dynamic_slice_in_dim(own, odd * last, face, 1), "slab", False)
    high = lax.reduce_precision(info, 8, 7)
    middle = lax.reduce_precision(info - high, 8, 7)
    parts = [x.astype(BF16) for x in (high, middle, info - high - middle)]
    near, far = near.reshape(-1, channels), far.reshape(-1, channels)
    faces = jnp.concatenate([near, far, *parts], axis=0)
    bits = [1 << b for b in reversed(range((plane - 1).bit_length()))]
    held = {0: (own, faces)}
    for bit in bits:
        for j in list(held):
            held[j ^ bit] = tuple(partner(x, "xy", bit) for x in held[j])
    pieces = [held[j] for j in range(plane)]

    first = me * part
    mix_part = lax.dynamic_slice_in_dim(mix_weight, first, part, axis=2)
    mix_part = jnp.transpose(mix_part, (0, 2, 1))
    pick = lax.broadcasted_iota(jnp.int32, (4, part, channels), 1) + first
    pick = (pick == lax.broadcasted_iota(jnp.int32, (4, part, channels), 2)).astype(BF16)
    mix_part = jnp.concatenate([mix_part, pick], axis=1)
    gate_part = lax.dynamic_slice_in_dim(gate_weight.reshape(channels, 3, channels), first, part, axis=2)
    gate_part = jnp.transpose(gate_part, (1, 2, 0)).reshape(3 * part, channels)
    radial_part = lax.dynamic_slice_in_dim(radial_weight.reshape(nbasis, 4, channels), first, part, axis=2)
    radial_part = jnp.transpose(radial_part, (1, 2, 0)).reshape(4 * part, nbasis)
    high = lax.reduce_precision(radial_part, 8, 7)
    three = jnp.stack([high, high, radial_part - high], axis=1)
    same = jnp.eye(slots, dtype=F32)
    radial_lhs = three[None, :, :, :, None] * same[:, None, None, None, :]
    radial_lhs = radial_lhs.reshape(slots * 4 * part, 3 * nbasis * slots).astype(BF16)
    out_part = lax.dynamic_slice_in_dim(out_weight, first, part)[:, None]

    coef, harm, column, goals = call(
        functools.partial(geometry_kernel, slots, atoms, edge, plane),
        (
            jax.ShapeDtypeStruct((slots * 4 * part, lanes), F32),
            jax.ShapeDtypeStruct((harm_count * slots, lanes), F32),
            jax.ShapeDtypeStruct((slots, lanes), jnp.int32),
            jax.ShapeDtypeStruct((slots, lanes), F32),
        ),
        [],
        place,
        *[p[1] for p in pieces],
        radial_lhs,
    )
    feats, mixed, gates, message, dens = call(
        functools.partial(forward_kernel, slots, plane),
        (
            jax.ShapeDtypeStruct((harm_count, total, channels), BF16),
            jax.ShapeDtypeStruct((harm_count * part, total), F32),
            jax.ShapeDtypeStruct((3 * part, total), F32),
            jax.ShapeDtypeStruct((part, lanes), F32),
            jax.ShapeDtypeStruct((8, lanes), F32),
        ),
        [pltpu.VMEM((harm_count * part, total), BF16)],
        *[p[0] for p in pieces],
        *[p[1] for p in pieces],
        coef,
        harm,
        column,
        mix_part,
        gate_part,
        out_part,
    )
    dens_all = [dens] + [partner(dens, "xy", j) for j in range(1, plane)]

    groups = [1] + [1 << b for b in range((plane - 1).bit_length())]
    outs = call(
        functools.partial(backward_kernel, slots, plane, 1.0 / float(slabs * plane), float(probes)),
        (
            jax.ShapeDtypeStruct((7 * part, channels), F32),
            jax.ShapeDtypeStruct((8, probes), F32),
        )
        + tuple(jax.ShapeDtypeStruct((rows * (atoms + edge), harm_count * part), BF16) for rows in groups),
        [pltpu.VMEM((harm_count * part, total), F32)],
        *dens_all,
        coef,
        harm,
        column,
        goals,
        feats,
        mixed,
        gates,
        message,
        out_part,
    )
    weight, density, sends = outs[0], outs[1], list(outs[2:])

    steps = [1 << b for b in range((slabs - 1).bit_length())]
    size = atoms + edge
    entries = [(0, sends[0], {0: 0})]
    for b, block in enumerate(sends[1:]):
        entries.append((0, block, {j: (j - (1 << b)) * size for j in range(1 << b, 2 << b)}))
    for bit in bits:
        due = [e for e in entries if any(bit <= j < 2 * bit for j in e[2])]
        for source, block, places in due:
            moved = {j ^ bit: at for j, at in places.items()}
            entries.append((source ^ bit, partner(block, "xy", bit), moved))
    mine = {source: (block, places[0]) for source, block, places in entries if 0 in places}
    slices = [mine[j][0] for j in range(plane)]
    firsts = tuple(mine[j][1] for j in range(plane))
    for bit in steps[:-1]:
        weight = weight + partner(weight, "slab", bit)
    weight = weight.astype(LAST_STEP)
    weight, *slices = lax.optimization_barrier((weight, *slices))
    weight = (weight, partner(weight, "slab", steps[-1]))
    edges = [s[f + atoms : f + size] for s, f in zip(slices, firsts)]
    near_grad = beside(jnp.stack([e[:face] for e in edges], axis=0), "slab", True)
    far_grad = beside(jnp.stack([e[face:] for e in edges], axis=0), "slab", False)
    *weight, near_grad, far_grad = lax.optimization_barrier((*weight, near_grad, far_grad))
    weight = weight[0].astype(F32) + weight[1].astype(F32)
    feat_grad = call(
        functools.partial(finish_kernel, plane, firsts),
        jax.ShapeDtypeStruct((atoms, harm_count, channels), F32),
        [],
        place,
        *slices,
        near_grad,
        far_grad,
        own,
        mix_weight,
        gate_weight,
    )

    columns = {0: weight}
    for bit in bits:
        arrived = {j ^ bit: partner(columns[j], "xy", bit) for j in columns}
        if bit == bits[0]:
            *values, feat_grad = lax.optimization_barrier((*arrived.values(), feat_grad))
            arrived = dict(zip(arrived, values))
        columns.update(arrived)
    mix_grad, gate_grad = call(
        functools.partial(assemble_kernel, plane),
        (
            jax.ShapeDtypeStruct((4, channels, channels), F32),
            jax.ShapeDtypeStruct((channels, 3 * channels), F32),
        ),
        [pltpu.VMEM((7, channels, channels), F32)],
        place,
        *[columns[j] for j in range(plane)],
    )
    return (density[0], feat_grad, mix_grad, gate_grad)


def solution(mesh):
    in_specs = (
        P(("slab", "xy"), None, None),
        P(),
        P(),
        P(),
        P(),
        P(None, None, ("slab", "xy")),
        P(None, ("slab", "xy")),
        P(("slab", "xy")),
        P(("slab", "xy")),
    )
    out_specs = (P(("slab", "xy")), P(("slab", "xy"), None, None), P(), P())
    return jax.shard_map(body, mesh=mesh, in_specs=in_specs, out_specs=out_specs, check_vma=False)
```

```python
import functools
import math

import jax
import jax.numpy as jnp
from jax import lax
from jax.experimental import pallas as pl
from jax.experimental.pallas import tpu as pltpu
from jax.sharding import PartitionSpec as P

DEGREE_SPANS = ((0, 1), (1, 4), (4, 9), (9, 16))
DEGREE_OF = (0,) + (1,) * 3 + (2,) * 5 + (3,) * 7
HARM = 16
SPACING = 0.35
root_three = math.sqrt(3.0)
cubic_outer = math.sqrt(10.0) / 4.0
cubic_middle = math.sqrt(15.0)
cubic_inner = math.sqrt(6.0) / 4.0
VMEM_BYTES = 20 * 2**20
F32 = jnp.float32
BF16 = jnp.bfloat16


def harmonics(x, y, z):
    r2 = x * x + y * y + z * z
    terms = [
        None,
        x,
        y,
        z,
        root_three * x * y,
        root_three * y * z,
        0.5 * (3.0 * z * z - r2),
        root_three * x * z,
        0.5 * root_three * (x * x - y * y),
        cubic_outer * y * (3.0 * x * x - y * y),
        cubic_middle * x * y * z,
        cubic_inner * y * (5.0 * z * z - r2),
        0.5 * z * (5.0 * z * z - 3.0 * r2),
        cubic_inner * x * (5.0 * z * z - r2),
        0.5 * cubic_middle * z * (x * x - y * y),
        cubic_outer * x * (x * x - 3.0 * y * y),
    ]
    return terms, r2


def split_high_low(values):
    high = values.astype(BF16)
    return high, (values - high.astype(F32)).astype(BF16)


def dot_lanes(left, right):
    return lax.dot_general(left, right, (((1,), (1,)), ((), ())), preferred_element_type=F32)


def dot(left, right):
    return jnp.dot(left, right, preferred_element_type=F32)


def partner(block, axis, bit):
    count = lax.axis_size(axis)
    return lax.ppermute(block, axis, [(i, i ^ bit) for i in range(count)])


def inner(block, axis):
    count = lax.axis_size(axis)
    pairs = [(i, i + 1) for i in range(1, count - 1, 2)]
    return lax.ppermute(block, axis, pairs + [(j, i) for i, j in pairs])


def beside(block, axis, first):
    count = lax.axis_size(axis)
    pairs = [(i, (i + 1) % count) for i in range(0 if first else 1, count, 2)]
    return lax.ppermute(block, axis, pairs + [(j, i) for i, j in pairs])


def table(column_ref, k, total):
    column = column_ref[k : k + 1, :]
    rows = lax.broadcasted_iota(jnp.int32, (total, column.shape[1]), 0)
    return jnp.where(rows == column, 1.0, 0.0).astype(BF16)


def geometry_kernel(slots, atoms, edge, plane, place_ref, *refs):
    rows_of = (refs[0].shape[0] - HARM * edge) // 3
    info = [
        sum(ref[HARM * edge + i * rows_of : HARM * edge + (i + 1) * rows_of, :].astype(F32) for i in range(3))
        for ref in refs[:plane]
    ]
    lhs_ref, coef_ref, harm_ref, column_ref, target_ref = refs[plane:]

    def rows(first):
        return jnp.concatenate([x[first * slots : (first + 1) * slots, :] for x in info], axis=1)

    harm, r2 = harmonics(rows(0), rows(1), rows(2))
    for lm in range(1, HARM):
        harm_ref[lm * slots : (lm + 1) * slots, :] = harm[lm]
    harm_ref[:slots, :] = jnp.ones_like(r2)
    code = rows(3).astype(jnp.int32)
    tail = rows(4)
    target_ref[...] = tail
    slot = lax.broadcasted_iota(jnp.int32, code.shape, 0).astype(F32)
    active = (slot < tail[0:1, :]).astype(F32)
    relative = (code & (plane - 1)) ^ (place_ref[0] >> 1)
    offset = code >> (plane.bit_length() - 1)
    column_ref[...] = offset + relative * jnp.where(offset < plane * atoms, atoms, edge)
    envelope = (1.0 - r2 / 7.0) ** 2 * active
    distance = jnp.sqrt(r2)
    nbasis = lhs_ref.shape[1] // (3 * slots)
    values = [jnp.exp(-(((distance - SPACING * b) / SPACING) ** 2)) * envelope for b in range(nbasis)]
    high, low = split_high_low(jnp.concatenate(values, axis=0))
    coef_ref[...] = dot(lhs_ref[...], jnp.concatenate([high, low, high], axis=0))


def forward_kernel(slots, plane, *refs):
    wide = refs[:plane]
    faces = refs[plane : 2 * plane]
    coef_ref, harm_ref, column_ref, mix_ref, gate_ref, out_w_ref = refs[2 * plane : 2 * plane + 6]
    feats_ref, mixed_ref, gates_ref, msg_ref, dens_ref, source_ref = refs[2 * plane + 6 :]
    atoms = wide[0].shape[1]
    edge = (feats_ref.shape[1] - plane * atoms) // plane
    face = edge // 2
    total = plane * (atoms + edge)
    part = mix_ref.shape[1] // 2
    for j in range(plane):
        feats_ref[:, j * atoms : (j + 1) * atoms, :] = wide[j][...]
        for side in range(2):
            at = plane * atoms + j * edge + side * face
            for lm in range(HARM):
                first = (side * HARM + lm) * face
                feats_ref[lm, at : at + face, :] = faces[j][first : first + face, :]
    gates_ref[...] = jax.nn.sigmoid(dot_lanes(gate_ref[...], feats_ref[0]))
    for lm in range(HARM):
        degree = DEGREE_OF[lm]
        both = dot_lanes(mix_ref[degree], feats_ref[lm])
        mixed, plain = both[:part], both[part:]
        mixed_ref[lm * part : (lm + 1) * part, :] = mixed
        if degree == 0:
            update = mixed * jax.nn.sigmoid(mixed)
        else:
            update = mixed * gates_ref[(degree - 1) * part : degree * part, :]
        source_ref[lm * part : (lm + 1) * part, :] = (plain + update).astype(BF16)
    message = jnp.zeros(msg_ref.shape, F32)
    for k in range(slots):
        rows = dot(source_ref[...], table(column_ref, k, total))
        for degree, (start, end) in enumerate(DEGREE_SPANS):
            inner = None
            for lm in range(start, end):
                term = rows[lm * part : (lm + 1) * part]
                if lm > 0:
                    term = term * harm_ref[lm * slots + k : lm * slots + k + 1, :]
                inner = term if inner is None else inner + term
            at = (k * 4 + degree) * part
            message = message + inner * coef_ref[at : at + part, :]
    msg_ref[...] = message
    partial = jnp.sum(message * jax.nn.sigmoid(message) * out_w_ref[...], axis=0, keepdims=True)
    dens_ref[...] = jnp.broadcast_to(partial, dens_ref.shape)


def backward_kernel(slots, plane, scale, probes_dev, *refs):
    dens = refs[:plane]
    coef_ref, harm_ref, column_ref, target_ref, feats_ref = refs[plane : plane + 5]
    mixed_ref, gates_ref, msg_ref, out_w_ref = refs[plane + 5 : plane + 9]
    weight_ref, density_ref = refs[plane + 9 : plane + 11]
    send_refs = refs[plane + 11 : -1]
    grad_ref = refs[-1]
    part = msg_ref.shape[0]
    total = feats_ref.shape[1]
    rows_out = send_refs[0].shape[0]
    atoms = 2 * rows_out // 3
    edge = rows_out - atoms
    probes = msg_ref.shape[1] // plane
    density = dens[0][0:1, :]
    for j in range(1, plane):
        other = dens[j][0:1, :]
        density = density + jnp.concatenate(
            [other[:, (b ^ j) * probes : ((b ^ j) + 1) * probes] for b in range(plane)], axis=1
        )
    density_ref[...] = jnp.broadcast_to(density[:, :probes], density_ref.shape)
    d_density = (density - target_ref[1:2, :]) * (1.0 / probes_dev)
    message = msg_ref[...]
    sig = jax.nn.sigmoid(message)
    d_message = d_density * out_w_ref[...] * (sig * (1.0 + message * (1.0 - sig)))
    for k in range(slots):
        pieces = []
        for degree, (start, end) in enumerate(DEGREE_SPANS):
            at = (k * 4 + degree) * part
            base = coef_ref[at : at + part, :] * d_message
            for lm in range(start, end):
                piece = base if lm == 0 else base * harm_ref[lm * slots + k : lm * slots + k + 1, :]
                pieces.append(piece.astype(BF16))
        contribution = jnp.concatenate(pieces, axis=0)
        product = dot_lanes(contribution, table(column_ref, k, total))
        if k == 0:
            grad_ref[...] = product
        else:
            grad_ref[...] += product
    for degree, (start, end) in enumerate(DEGREE_SPANS):
        sums = None
        gate_sum = None
        for lm in range(start, end):
            grad = grad_ref[lm * part : (lm + 1) * part, :]
            mixed = mixed_ref[lm * part : (lm + 1) * part, :]
            if degree == 0:
                s = jax.nn.sigmoid(mixed)
                d_mixed = grad * (s * (1.0 + mixed * (1.0 - s)))
            else:
                d_mixed = grad * gates_ref[(degree - 1) * part : degree * part, :]
                gate_sum = grad * mixed if gate_sum is None else gate_sum + grad * mixed
            high, low = split_high_low(d_mixed)
            product = dot(jnp.concatenate([high, low], axis=0), feats_ref[lm])
            sums = product if sums is None else sums + product
        weight_ref[degree * part : (degree + 1) * part, :] = (sums[:part] + sums[part:]) * scale
        if degree > 0:
            gates = gates_ref[(degree - 1) * part : degree * part, :]
            high, low = split_high_low(gate_sum * gates * (1.0 - gates))
            product = dot(jnp.concatenate([high, low], axis=0), feats_ref[0])
            at = (3 + degree) * part
            weight_ref[at : at + part, :] = (product[:part] + product[part:]) * scale
    turned = grad_ref[...].T
    for j in range(plane):
        send_ref = send_refs[j.bit_length()]
        first = (j - (1 << j.bit_length() >> 1)) * rows_out
        send_ref[first : first + atoms, :] = turned[j * atoms : (j + 1) * atoms].astype(BF16)
        at = plane * atoms + j * edge
        send_ref[first + atoms : first + rows_out, :] = turned[at : at + edge].astype(BF16)


def finish_kernel(plane, firsts, place_ref, *refs):
    slices = refs[:plane]
    near_ref, far_ref, feats_ref, mix_ref, gate_ref, out_ref = refs[plane:]
    atoms = feats_ref.shape[1]
    channels = feats_ref.shape[2]
    part = channels // plane
    face = near_ref.shape[1]
    odd = (jnp.zeros((face, channels), jnp.int32) + place_ref[0]) % 2 > 0
    per = channels // part
    me = place_ref[0] >> 1
    lane = lax.broadcasted_iota(jnp.int32, (atoms, channels), 1)
    gates = jax.nn.sigmoid(dot(feats_ref[0], gate_ref[...]))

    def slab(j, group):
        columns = slice(group * channels, (group + 1) * channels)
        own = slices[j][firsts[j] : firsts[j] + atoms, columns].astype(F32)
        near, far = near_ref[j, :, columns].astype(F32), far_ref[j, :, columns].astype(F32)
        low = own[:face] + jnp.where(odd, near, far)
        high = own[atoms - face :] + jnp.where(odd, far, near)
        return jnp.concatenate([low, own[face : atoms - face], high], axis=0)

    upstream = []
    for group in range(HARM // per):
        blocks = [slab(j, group) for j in range(plane)]
        for place in range(per):
            total = None
            for j in range(plane):
                home = (me ^ j) * part
                shift = (home - place * part + channels) % channels
                moved = pltpu.roll(blocks[j], shift, 1)
                keep = jnp.where((lane >= home) & (lane < home + part), moved, 0.0)
                total = keep if total is None else total + keep
            upstream.append(total)
    gate_parts = []
    zero_row = None
    for degree, (start, end) in enumerate(DEGREE_SPANS):
        weight = mix_ref[degree]
        gate_sum = None
        for lm in range(start, end):
            mixed = dot(feats_ref[lm], weight)
            if degree == 0:
                s = jax.nn.sigmoid(mixed)
                d_mixed = upstream[lm] * (s * (1.0 + mixed * (1.0 - s)))
            else:
                d_mixed = upstream[lm] * gates[:, (degree - 1) * channels : degree * channels]
                product = upstream[lm] * mixed
                gate_sum = product if gate_sum is None else gate_sum + product
            high, low = split_high_low(d_mixed)
            back = dot_lanes(jnp.concatenate([high, low], axis=0), weight)
            result = upstream[lm] + back[:atoms] + back[atoms:]
            if degree == 0:
                zero_row = result
            else:
                out_ref[:, lm, :] = result
        if degree > 0:
            gate_parts.append(gate_sum)
    d_gate = jnp.concatenate(gate_parts, axis=1) * gates * (1.0 - gates)
    high, low = split_high_low(d_gate)
    back = dot_lanes(jnp.concatenate([high, low], axis=0), gate_ref[...])
    out_ref[:, 0, :] = zero_row + back[:atoms] + back[atoms:]


def assemble_kernel(plane, place_ref, *refs):
    pieces = refs[:plane]
    mix_ref, gate_ref = refs[plane : plane + 2]
    (joined_ref,) = refs[plane + 2 :]
    part = pieces[0].shape[0] // 7
    channels = plane * part
    for j in range(plane):
        home = pl.multiple_of(((place_ref[0] >> 1) ^ j) * part, part)
        for block in range(7):
            joined_ref[block, pl.ds(home, part), :] = pieces[j][block * part : (block + 1) * part, :]
    for block in range(4):
        mix_ref[block] = joined_ref[block].T
    for block in range(3):
        gate_ref[:, block * channels : (block + 1) * channels] = joined_ref[4 + block].T


def call(kernel, outs, scratch, *arrays):
    vmem = pl.BlockSpec(memory_space=pltpu.VMEM)
    smem = pl.BlockSpec(memory_space=pltpu.SMEM)
    return pl.pallas_call(
        kernel,
        out_shape=outs,
        in_specs=[smem if x.shape == (1,) else vmem for x in arrays],
        out_specs=jax.tree.map(lambda _: vmem, outs),
        scratch_shapes=scratch,
        compiler_params=pltpu.CompilerParams(vmem_limit_bytes=VMEM_BYTES),
    )(*arrays)


def body(
    atom_feats,
    mix_weight,
    gate_weight,
    radial_weight,
    out_weight,
    pair_vec,
    nbr_atom,
    nbr_count,
    target,
):
    atoms, harm_count, channels = atom_feats.shape
    slots, probes = nbr_atom.shape
    nbasis = radial_weight.shape[0]
    plane = lax.axis_size("xy")
    slabs = lax.axis_size("slab")
    part = channels // plane
    face = atoms // 4
    edge = 2 * face
    total = plane * (atoms + edge)
    lanes = plane * probes
    me = lax.axis_index("xy").astype(jnp.int32)
    slab = lax.axis_index("slab").astype(jnp.int32)
    odd = slab % 2
    place = (me * 2 + odd)[None]

    domain = nbr_atom // atoms
    row = nbr_atom % atoms
    step = domain // plane - slab
    wide = plane * atoms
    below = wide + (1 - odd) * face + row - (atoms - face)
    above = wide + odd * face + row
    offset = jnp.where(step == 0, row, jnp.where(step < 0, below, above))
    code = offset * plane + domain % plane
    tail = jnp.concatenate(
        [nbr_count.astype(F32)[None], target[None], jnp.zeros((2 * slots - 2, probes), F32)], axis=0
    )
    info = jnp.concatenate([pair_vec.reshape(3 * slots, probes), code.astype(F32), tail], axis=0)

    own = jnp.transpose(atom_feats, (1, 0, 2))
    last = atoms - face
    near = beside(lax.dynamic_slice_in_dim(own, (1 - odd) * last, face, 1), "slab", True)
    far = beside(lax.dynamic_slice_in_dim(own, odd * last, face, 1), "slab", False)
    high = lax.reduce_precision(info, 8, 7)
    middle = lax.reduce_precision(info - high, 8, 7)
    parts = [x.astype(BF16) for x in (high, middle, info - high - middle)]
    near, far = near.reshape(-1, channels), far.reshape(-1, channels)
    faces = jnp.concatenate([near, far, *parts], axis=0)
    bits = [1 << b for b in reversed(range((plane - 1).bit_length()))]
    held = {0: (own, faces)}
    for bit in bits:
        for j in list(held):
            held[j ^ bit] = tuple(partner(x, "xy", bit) for x in held[j])
    pieces = [held[j] for j in range(plane)]

    first = me * part
    mix_part = lax.dynamic_slice_in_dim(mix_weight, first, part, axis=2)
    mix_part = jnp.transpose(mix_part, (0, 2, 1))
    pick = lax.broadcasted_iota(jnp.int32, (4, part, channels), 1) + first
    pick = (pick == lax.broadcasted_iota(jnp.int32, (4, part, channels), 2)).astype(BF16)
    mix_part = jnp.concatenate([mix_part, pick], axis=1)
    gate_part = lax.dynamic_slice_in_dim(gate_weight.reshape(channels, 3, channels), first, part, axis=2)
    gate_part = jnp.transpose(gate_part, (1, 2, 0)).reshape(3 * part, channels)
    radial_part = lax.dynamic_slice_in_dim(radial_weight.reshape(nbasis, 4, channels), first, part, axis=2)
    radial_part = jnp.transpose(radial_part, (1, 2, 0)).reshape(4 * part, nbasis)
    high = lax.reduce_precision(radial_part, 8, 7)
    three = jnp.stack([high, high, radial_part - high], axis=1)
    same = jnp.eye(slots, dtype=F32)
    radial_lhs = three[None, :, :, :, None] * same[:, None, None, None, :]
    radial_lhs = radial_lhs.reshape(slots * 4 * part, 3 * nbasis * slots).astype(BF16)
    out_part = lax.dynamic_slice_in_dim(out_weight, first, part)[:, None]

    coef, harm, column, goals = call(
        functools.partial(geometry_kernel, slots, atoms, edge, plane),
        (
            jax.ShapeDtypeStruct((slots * 4 * part, lanes), F32),
            jax.ShapeDtypeStruct((harm_count * slots, lanes), F32),
            jax.ShapeDtypeStruct((slots, lanes), jnp.int32),
            jax.ShapeDtypeStruct((slots, lanes), F32),
        ),
        [],
        place,
        *[p[1] for p in pieces],
        radial_lhs,
    )
    feats, mixed, gates, message, dens = call(
        functools.partial(forward_kernel, slots, plane),
        (
            jax.ShapeDtypeStruct((harm_count, total, channels), BF16),
            jax.ShapeDtypeStruct((harm_count * part, total), F32),
            jax.ShapeDtypeStruct((3 * part, total), F32),
            jax.ShapeDtypeStruct((part, lanes), F32),
            jax.ShapeDtypeStruct((8, lanes), F32),
        ),
        [pltpu.VMEM((harm_count * part, total), BF16)],
        *[p[0] for p in pieces],
        *[p[1] for p in pieces],
        coef,
        harm,
        column,
        mix_part,
        gate_part,
        out_part,
    )
    dens_all = [dens] + [partner(dens, "xy", j) for j in range(1, plane)]

    groups = [1] + [1 << b for b in range((plane - 1).bit_length())]
    outs = call(
        functools.partial(backward_kernel, slots, plane, 1.0 / float(slabs * plane), float(probes)),
        (
            jax.ShapeDtypeStruct((7 * part, channels), F32),
            jax.ShapeDtypeStruct((8, probes), F32),
        )
        + tuple(jax.ShapeDtypeStruct((rows * (atoms + edge), harm_count * part), BF16) for rows in groups),
        [pltpu.VMEM((harm_count * part, total), F32)],
        *dens_all,
        coef,
        harm,
        column,
        goals,
        feats,
        mixed,
        gates,
        message,
        out_part,
    )
    weight, density, sends = outs[0], outs[1], list(outs[2:])

    steps = [1 << b for b in range((slabs - 1).bit_length())]
    size = atoms + edge
    entries = [(0, sends[0], {0: 0})]
    for b, block in enumerate(sends[1:]):
        entries.append((0, block, {j: (j - (1 << b)) * size for j in range(1 << b, 2 << b)}))
    for bit in bits:
        due = [e for e in entries if any(bit <= j < 2 * bit for j in e[2])]
        for source, block, places in due:
            moved = {j ^ bit: at for j, at in places.items()}
            entries.append((source ^ bit, partner(block, "xy", bit), moved))
    mine = {source: (block, places[0]) for source, block, places in entries if 0 in places}
    slices = [mine[j][0] for j in range(plane)]
    firsts = tuple(mine[j][1] for j in range(plane))
    for bit in steps[:-2]:
        weight = weight + partner(weight, "slab", bit)
    weight = weight.astype(BF16)
    one, two = steps[-2:]
    weight = [weight] + [partner(weight, "slab", bit) for bit in (one, two, one + two)]
    *weight, last_slice = lax.optimization_barrier((*weight, slices[-1]))
    slices = slices[:-1] + [last_slice]
    edges = [s[f + atoms : f + size] for s, f in zip(slices, firsts)]
    near_grad = beside(jnp.stack([e[:face] for e in edges], axis=0), "slab", True)
    far_grad = inner(jnp.stack([e[face:] for e in edges], axis=0), "slab")
    near_sum = weight[0].astype(F32) + weight[1].astype(F32)
    weight = near_sum + (weight[2].astype(F32) + weight[3].astype(F32))
    columns = {0: weight}
    for bit in bits:
        arrived = {j ^ bit: partner(columns[j], "xy", bit) for j in columns}
        columns.update(arrived)
    mix_grad, gate_grad = call(
        functools.partial(assemble_kernel, plane),
        (
            jax.ShapeDtypeStruct((4, channels, channels), F32),
            jax.ShapeDtypeStruct((channels, 3 * channels), F32),
        ),
        [pltpu.VMEM((7, channels, channels), F32)],
        place,
        *[columns[j] for j in range(plane)],
    )
    mix_grad, gate_grad, near_grad, far_grad = lax.optimization_barrier((mix_grad, gate_grad, near_grad, far_grad))
    feat_grad = call(
        functools.partial(finish_kernel, plane, firsts),
        jax.ShapeDtypeStruct((atoms, harm_count, channels), F32),
        [],
        place,
        *slices,
        near_grad,
        far_grad,
        own,
        mix_weight,
        gate_weight,
    )
    return (density[0], feat_grad, mix_grad, gate_grad)


def solution(mesh):
    in_specs = (
        P(("slab", "xy"), None, None),
        P(),
        P(),
        P(),
        P(),
        P(None, None, ("slab", "xy")),
        P(None, ("slab", "xy")),
        P(("slab", "xy")),
        P(("slab", "xy")),
    )
    out_specs = (P(("slab", "xy")), P(("slab", "xy"), None, None), P(), P())
    return jax.shard_map(body, mesh=mesh, in_specs=in_specs, out_specs=out_specs, check_vma=False)
```

```python
import functools
import math

import jax
import jax.numpy as jnp
from jax import lax
from jax.experimental import pallas as pl
from jax.experimental.pallas import tpu as pltpu
from jax.sharding import PartitionSpec as P

DEGREE_SPANS = ((0, 1), (1, 4), (4, 9), (9, 16))
DEGREE_OF = (0,) + (1,) * 3 + (2,) * 5 + (3,) * 7
HARM = 16
SPACING = 0.35
root_three = math.sqrt(3.0)
cubic_outer = math.sqrt(10.0) / 4.0
cubic_middle = math.sqrt(15.0)
cubic_inner = math.sqrt(6.0) / 4.0
VMEM_BYTES = 20 * 2**20
F32 = jnp.float32
BF16 = jnp.bfloat16


def harmonics(x, y, z):
    r2 = x * x + y * y + z * z
    terms = [
        None,
        x,
        y,
        z,
        root_three * x * y,
        root_three * y * z,
        0.5 * (3.0 * z * z - r2),
        root_three * x * z,
        0.5 * root_three * (x * x - y * y),
        cubic_outer * y * (3.0 * x * x - y * y),
        cubic_middle * x * y * z,
        cubic_inner * y * (5.0 * z * z - r2),
        0.5 * z * (5.0 * z * z - 3.0 * r2),
        cubic_inner * x * (5.0 * z * z - r2),
        0.5 * cubic_middle * z * (x * x - y * y),
        cubic_outer * x * (x * x - 3.0 * y * y),
    ]
    return terms, r2


def split_high_low(values):
    high = values.astype(BF16)
    return high, (values - high.astype(F32)).astype(BF16)


def dot_lanes(left, right):
    return lax.dot_general(left, right, (((1,), (1,)), ((), ())), preferred_element_type=F32)


def dot(left, right):
    return jnp.dot(left, right, preferred_element_type=F32)


def partner(block, axis, bit):
    count = lax.axis_size(axis)
    return lax.ppermute(block, axis, [(i, i ^ bit) for i in range(count)])


def inner(block, axis):
    count = lax.axis_size(axis)
    pairs = [(i, i + 1) for i in range(1, count - 1, 2)]
    return lax.ppermute(block, axis, pairs + [(j, i) for i, j in pairs])


def beside(block, axis, first):
    count = lax.axis_size(axis)
    pairs = [(i, (i + 1) % count) for i in range(0 if first else 1, count, 2)]
    return lax.ppermute(block, axis, pairs + [(j, i) for i, j in pairs])


def table(column_ref, k, total):
    column = column_ref[k : k + 1, :]
    rows = lax.broadcasted_iota(jnp.int32, (total, column.shape[1]), 0)
    return jnp.where(rows == column, 1.0, 0.0).astype(BF16)


def pair_geometry(slots, atoms, edge, plane, place_ref, faces, lhs_ref, coef_ref, harm_ref, column_ref, target_ref):
    groups = (faces[0].shape[0] - 2 * HARM) // 3
    info = []
    for ref in faces:
        parts = [ref[2 * HARM + i * groups : 2 * HARM + (i + 1) * groups].astype(F32) for i in range(3)]
        info.append((parts[0] + parts[1] + parts[2]).reshape(groups * ref.shape[1], -1))

    def rows(first):
        return jnp.concatenate([x[first * slots : (first + 1) * slots, :] for x in info], axis=1)

    harm, r2 = harmonics(rows(0), rows(1), rows(2))
    for lm in range(1, HARM):
        harm_ref[lm * slots : (lm + 1) * slots, :] = harm[lm]
    harm_ref[:slots, :] = jnp.ones_like(r2)
    code = rows(3).astype(jnp.int32)
    tail = rows(4)
    target_ref[...] = tail
    slot = lax.broadcasted_iota(jnp.int32, code.shape, 0).astype(F32)
    active = (slot < tail[0:1, :]).astype(F32)
    relative = (code & (plane - 1)) ^ (place_ref[0] >> 1)
    offset = code >> (plane.bit_length() - 1)
    column_ref[...] = offset + relative * jnp.where(offset < plane * atoms, atoms, edge)
    envelope = (1.0 - r2 / 7.0) ** 2 * active
    distance = jnp.sqrt(r2)
    nbasis = lhs_ref.shape[1] // (3 * slots)
    values = [jnp.exp(-(((distance - SPACING * b) / SPACING) ** 2)) * envelope for b in range(nbasis)]
    high, low = split_high_low(jnp.concatenate(values, axis=0))
    coef_ref[...] = dot(lhs_ref[...], jnp.concatenate([high, low, high], axis=0))


def forward_kernel(slots, plane, place_ref, *refs):
    wide = refs[:plane]
    faces = refs[plane : 2 * plane]
    lhs_ref, mix_ref, gate_ref, out_w_ref = refs[2 * plane : 2 * plane + 4]
    feats_ref, mixed_ref, gates_ref, msg_ref, dens_ref = refs[2 * plane + 4 : 2 * plane + 9]
    coef_ref, harm_ref, column_ref, target_ref, source_ref = refs[2 * plane + 9 :]
    atoms = wide[0].shape[1]
    edge = (feats_ref.shape[1] - plane * atoms) // plane
    face = edge // 2
    total = plane * (atoms + edge)
    part = mix_ref.shape[1] // 2
    for j in range(plane):
        feats_ref[:, j * atoms : (j + 1) * atoms, :] = wide[j][...]
        for side in range(2):
            at = plane * atoms + j * edge + side * face
            feats_ref[:, at : at + face, :] = faces[j][side * HARM : (side + 1) * HARM]
    pair_geometry(slots, atoms, edge, plane, place_ref, faces, lhs_ref, coef_ref, harm_ref, column_ref, target_ref)
    gates_ref[...] = jax.nn.sigmoid(dot_lanes(gate_ref[...], feats_ref[0]))
    for lm in range(HARM):
        degree = DEGREE_OF[lm]
        both = dot_lanes(mix_ref[degree], feats_ref[lm])
        mixed, plain = both[:part], both[part:]
        mixed_ref[lm * part : (lm + 1) * part, :] = mixed
        if degree == 0:
            update = mixed * jax.nn.sigmoid(mixed)
        else:
            update = mixed * gates_ref[(degree - 1) * part : degree * part, :]
        source_ref[lm * part : (lm + 1) * part, :] = (plain + update).astype(BF16)
    message = jnp.zeros(msg_ref.shape, F32)
    for k in range(slots):
        rows = dot(source_ref[...], table(column_ref, k, total))
        for degree, (start, end) in enumerate(DEGREE_SPANS):
            inner = None
            for lm in range(start, end):
                term = rows[lm * part : (lm + 1) * part]
                if lm > 0:
                    term = term * harm_ref[lm * slots + k : lm * slots + k + 1, :]
                inner = term if inner is None else inner + term
            at = (k * 4 + degree) * part
            message = message + inner * coef_ref[at : at + part, :]
    msg_ref[...] = message
    partial = jnp.sum(message * jax.nn.sigmoid(message) * out_w_ref[...], axis=0, keepdims=True)
    dens_ref[...] = jnp.broadcast_to(partial, dens_ref.shape)


def backward_kernel(slots, plane, scale, probes_dev, *refs):
    dens = refs[:plane]
    coef_ref, harm_ref, column_ref, target_ref, feats_ref = refs[plane : plane + 5]
    mixed_ref, gates_ref, msg_ref, out_w_ref = refs[plane + 5 : plane + 9]
    weight_ref, density_ref = refs[plane + 9 : plane + 11]
    send_refs = refs[plane + 11 : -1]
    grad_ref = refs[-1]
    part = msg_ref.shape[0]
    total = feats_ref.shape[1]
    rows_out = send_refs[0].shape[0]
    atoms = 2 * rows_out // 3
    edge = rows_out - atoms
    probes = msg_ref.shape[1] // plane
    density = dens[0][0:1, :]
    for j in range(1, plane):
        other = dens[j][0:1, :]
        density = density + jnp.concatenate(
            [other[:, (b ^ j) * probes : ((b ^ j) + 1) * probes] for b in range(plane)], axis=1
        )
    density_ref[...] = jnp.broadcast_to(density[:, :probes], density_ref.shape)
    d_density = (density - target_ref[1:2, :]) * (1.0 / probes_dev)
    message = msg_ref[...]
    sig = jax.nn.sigmoid(message)
    d_message = d_density * out_w_ref[...] * (sig * (1.0 + message * (1.0 - sig)))
    for k in range(slots):
        pieces = []
        for degree, (start, end) in enumerate(DEGREE_SPANS):
            at = (k * 4 + degree) * part
            base = coef_ref[at : at + part, :] * d_message
            for lm in range(start, end):
                piece = base if lm == 0 else base * harm_ref[lm * slots + k : lm * slots + k + 1, :]
                pieces.append(piece.astype(BF16))
        contribution = jnp.concatenate(pieces, axis=0)
        product = dot_lanes(contribution, table(column_ref, k, total))
        if k == 0:
            grad_ref[...] = product
        else:
            grad_ref[...] += product
    for degree, (start, end) in enumerate(DEGREE_SPANS):
        sums = None
        gate_sum = None
        for lm in range(start, end):
            grad = grad_ref[lm * part : (lm + 1) * part, :]
            mixed = mixed_ref[lm * part : (lm + 1) * part, :]
            if degree == 0:
                s = jax.nn.sigmoid(mixed)
                d_mixed = grad * (s * (1.0 + mixed * (1.0 - s)))
            else:
                d_mixed = grad * gates_ref[(degree - 1) * part : degree * part, :]
                gate_sum = grad * mixed if gate_sum is None else gate_sum + grad * mixed
            high, low = split_high_low(d_mixed)
            product = dot(jnp.concatenate([high, low], axis=0), feats_ref[lm])
            sums = product if sums is None else sums + product
        weight_ref[degree * part : (degree + 1) * part, :] = (sums[:part] + sums[part:]) * scale
        if degree > 0:
            gates = gates_ref[(degree - 1) * part : degree * part, :]
            high, low = split_high_low(gate_sum * gates * (1.0 - gates))
            product = dot(jnp.concatenate([high, low], axis=0), feats_ref[0])
            at = (3 + degree) * part
            weight_ref[at : at + part, :] = (product[:part] + product[part:]) * scale
    turned = grad_ref[...].T
    for j in range(plane):
        send_ref = send_refs[j.bit_length()]
        first = (j - (1 << j.bit_length() >> 1)) * rows_out
        send_ref[first : first + atoms, :] = turned[j * atoms : (j + 1) * atoms].astype(BF16)
        at = plane * atoms + j * edge
        send_ref[first + atoms : first + rows_out, :] = turned[at : at + edge].astype(BF16)


def finish_kernel(plane, firsts, place_ref, *refs):
    slices = refs[:plane]
    near_ref, far_ref, feats_ref, mix_ref, gate_ref, out_ref = refs[plane:]
    atoms = feats_ref.shape[1]
    channels = feats_ref.shape[2]
    part = channels // plane
    face = near_ref.shape[1]
    odd = (jnp.zeros((face, channels), jnp.int32) + place_ref[0]) % 2 > 0
    per = channels // part
    me = place_ref[0] >> 1
    lane = lax.broadcasted_iota(jnp.int32, (atoms, channels), 1)
    gates = jax.nn.sigmoid(dot(feats_ref[0], gate_ref[...]))

    def slab(j, group):
        columns = slice(group * channels, (group + 1) * channels)
        own = slices[j][firsts[j] : firsts[j] + atoms, columns].astype(F32)
        near, far = near_ref[j, :, columns].astype(F32), far_ref[j, :, columns].astype(F32)
        low = own[:face] + jnp.where(odd, near, far)
        high = own[atoms - face :] + jnp.where(odd, far, near)
        return jnp.concatenate([low, own[face : atoms - face], high], axis=0)

    upstream = []
    for group in range(HARM // per):
        blocks = [slab(j, group) for j in range(plane)]
        for place in range(per):
            total = None
            for j in range(plane):
                home = (me ^ j) * part
                shift = (home - place * part + channels) % channels
                moved = pltpu.roll(blocks[j], shift, 1)
                keep = jnp.where((lane >= home) & (lane < home + part), moved, 0.0)
                total = keep if total is None else total + keep
            upstream.append(total)
    gate_parts = []
    zero_row = None
    for degree, (start, end) in enumerate(DEGREE_SPANS):
        weight = mix_ref[degree]
        mixed_all = dot(feats_ref[start:end].reshape(-1, channels), weight)
        gate_sum = None
        d_mixed = []
        for lm in range(start, end):
            mixed = mixed_all[(lm - start) * atoms : (lm - start + 1) * atoms]
            if degree == 0:
                s = jax.nn.sigmoid(mixed)
                d_mixed.append(upstream[lm] * (s * (1.0 + mixed * (1.0 - s))))
            else:
                d_mixed.append(upstream[lm] * gates[:, (degree - 1) * channels : degree * channels])
                product = upstream[lm] * mixed
                gate_sum = product if gate_sum is None else gate_sum + product
        high, low = split_high_low(jnp.concatenate(d_mixed, axis=0))
        rows = high.shape[0]
        back = dot_lanes(jnp.concatenate([high, low], axis=0), weight)
        back = back[:rows] + back[rows:]
        for lm in range(start, end):
            result = upstream[lm] + back[(lm - start) * atoms : (lm - start + 1) * atoms]
            if degree == 0:
                zero_row = result
            else:
                out_ref[:, lm, :] = result
        if degree > 0:
            gate_parts.append(gate_sum)
    d_gate = jnp.concatenate(gate_parts, axis=1) * gates * (1.0 - gates)
    high, low = split_high_low(d_gate)
    back = dot_lanes(jnp.concatenate([high, low], axis=0), gate_ref[...])
    out_ref[:, 0, :] = zero_row + back[:atoms] + back[atoms:]


def assemble_kernel(plane, place_ref, *refs):
    pieces = refs[:plane]
    mix_ref, gate_ref = refs[plane : plane + 2]
    (joined_ref,) = refs[plane + 2 :]
    part = pieces[0].shape[0] // 7
    channels = plane * part
    for j in range(plane):
        home = pl.multiple_of(((place_ref[0] >> 1) ^ j) * part, part)
        for block in range(7):
            joined_ref[block, pl.ds(home, part), :] = pieces[j][block * part : (block + 1) * part, :]
    for block in range(4):
        mix_ref[block] = joined_ref[block].T
    for block in range(3):
        gate_ref[:, block * channels : (block + 1) * channels] = joined_ref[4 + block].T


def call(kernel, outs, scratch, *arrays):
    vmem = pl.BlockSpec(memory_space=pltpu.VMEM)
    smem = pl.BlockSpec(memory_space=pltpu.SMEM)
    return pl.pallas_call(
        kernel,
        out_shape=outs,
        in_specs=[smem if x.shape == (1,) else vmem for x in arrays],
        out_specs=jax.tree.map(lambda _: vmem, outs),
        scratch_shapes=scratch,
        compiler_params=pltpu.CompilerParams(vmem_limit_bytes=VMEM_BYTES),
    )(*arrays)


def body(
    atom_feats,
    mix_weight,
    gate_weight,
    radial_weight,
    out_weight,
    pair_vec,
    nbr_atom,
    nbr_count,
    target,
):
    atoms, harm_count, channels = atom_feats.shape
    slots, probes = nbr_atom.shape
    nbasis = radial_weight.shape[0]
    plane = lax.axis_size("xy")
    slabs = lax.axis_size("slab")
    part = channels // plane
    face = atoms // 4
    edge = 2 * face
    total = plane * (atoms + edge)
    lanes = plane * probes
    me = lax.axis_index("xy").astype(jnp.int32)
    slab = lax.axis_index("slab").astype(jnp.int32)
    odd = slab % 2
    place = (me * 2 + odd)[None]

    domain = nbr_atom // atoms
    row = nbr_atom % atoms
    step = domain // plane - slab
    wide = plane * atoms
    below = wide + (1 - odd) * face + row - (atoms - face)
    above = wide + odd * face + row
    offset = jnp.where(step == 0, row, jnp.where(step < 0, below, above))
    code = offset * plane + domain % plane
    tail = jnp.concatenate(
        [nbr_count.astype(F32)[None], target[None], jnp.zeros((2 * slots - 2, probes), F32)], axis=0
    )
    info = jnp.concatenate([pair_vec.reshape(3 * slots, probes), code.astype(F32), tail], axis=0)

    own = jnp.transpose(atom_feats, (1, 0, 2))
    last = atoms - face
    near = beside(lax.dynamic_slice_in_dim(own, (1 - odd) * last, face, 1), "slab", True)
    far = beside(lax.dynamic_slice_in_dim(own, odd * last, face, 1), "slab", False)
    high = lax.reduce_precision(info, 8, 7)
    middle = lax.reduce_precision(info - high, 8, 7)
    parts = [x.astype(BF16) for x in (high, middle, info - high - middle)]
    faces = jnp.concatenate([near, far] + [x.reshape(-1, face, channels) for x in parts], axis=0)
    bits = [1 << b for b in reversed(range((plane - 1).bit_length()))]
    held = {0: (own, faces)}
    for bit in bits:
        for j in list(held):
            held[j ^ bit] = tuple(partner(x, "xy", bit) for x in held[j])
    pieces = [held[j] for j in range(plane)]

    first = me * part
    mix_part = lax.dynamic_slice_in_dim(mix_weight, first, part, axis=2)
    mix_part = jnp.transpose(mix_part, (0, 2, 1))
    pick = lax.broadcasted_iota(jnp.int32, (4, part, channels), 1) + first
    pick = (pick == lax.broadcasted_iota(jnp.int32, (4, part, channels), 2)).astype(BF16)
    mix_part = jnp.concatenate([mix_part, pick], axis=1)
    gate_part = lax.dynamic_slice_in_dim(gate_weight.reshape(channels, 3, channels), first, part, axis=2)
    gate_part = jnp.transpose(gate_part, (1, 2, 0)).reshape(3 * part, channels)
    radial_part = lax.dynamic_slice_in_dim(radial_weight.reshape(nbasis, 4, channels), first, part, axis=2)
    radial_part = jnp.transpose(radial_part, (1, 2, 0)).reshape(4 * part, nbasis)
    high = lax.reduce_precision(radial_part, 8, 7)
    three = jnp.stack([high, high, radial_part - high], axis=1)
    same = jnp.eye(slots, dtype=F32)
    radial_lhs = three[None, :, :, :, None] * same[:, None, None, None, :]
    radial_lhs = radial_lhs.reshape(slots * 4 * part, 3 * nbasis * slots).astype(BF16)
    out_part = lax.dynamic_slice_in_dim(out_weight, first, part)[:, None]

    feats, mixed, gates, message, dens, coef, harm, column, goals = call(
        functools.partial(forward_kernel, slots, plane),
        (
            jax.ShapeDtypeStruct((harm_count, total, channels), BF16),
            jax.ShapeDtypeStruct((harm_count * part, total), F32),
            jax.ShapeDtypeStruct((3 * part, total), F32),
            jax.ShapeDtypeStruct((part, lanes), F32),
            jax.ShapeDtypeStruct((8, lanes), F32),
            jax.ShapeDtypeStruct((slots * 4 * part, lanes), F32),
            jax.ShapeDtypeStruct((harm_count * slots, lanes), F32),
            jax.ShapeDtypeStruct((slots, lanes), jnp.int32),
            jax.ShapeDtypeStruct((slots, lanes), F32),
        ),
        [pltpu.VMEM((harm_count * part, total), BF16)],
        place,
        *[p[0] for p in pieces],
        *[p[1] for p in pieces],
        radial_lhs,
        mix_part,
        gate_part,
        out_part,
    )
    dens_all = [dens] + [partner(dens, "xy", j) for j in range(1, plane)]

    groups = [1] + [1 << b for b in range((plane - 1).bit_length())]
    outs = call(
        functools.partial(backward_kernel, slots, plane, 1.0 / float(slabs * plane), float(probes)),
        (
            jax.ShapeDtypeStruct((7 * part, channels), F32),
            jax.ShapeDtypeStruct((8, probes), F32),
        )
        + tuple(jax.ShapeDtypeStruct((rows * (atoms + edge), harm_count * part), BF16) for rows in groups),
        [pltpu.VMEM((harm_count * part, total), F32)],
        *dens_all,
        coef,
        harm,
        column,
        goals,
        feats,
        mixed,
        gates,
        message,
        out_part,
    )
    weight, density, sends = outs[0], outs[1], list(outs[2:])

    steps = [1 << b for b in range((slabs - 1).bit_length())]
    size = atoms + edge
    entries = [(0, sends[0], {0: 0})]
    for b, block in enumerate(sends[1:]):
        entries.append((0, block, {j: (j - (1 << b)) * size for j in range(1 << b, 2 << b)}))
    for bit in bits:
        due = [e for e in entries if any(bit <= j < 2 * bit for j in e[2])]
        for source, block, places in due:
            moved = {j ^ bit: at for j, at in places.items()}
            entries.append((source ^ bit, partner(block, "xy", bit), moved))
    mine = {source: (block, places[0]) for source, block, places in entries if 0 in places}
    slices = [mine[j][0] for j in range(plane)]
    firsts = tuple(mine[j][1] for j in range(plane))
    for bit in steps[:-2]:
        weight = weight + partner(weight, "slab", bit)
    weight = weight.astype(BF16)
    one, two = steps[-2:]
    weight = [weight] + [partner(weight, "slab", bit) for bit in (one, two, one + two)]
    *weight, last_slice = lax.optimization_barrier((*weight, slices[-1]))
    slices = slices[:-1] + [last_slice]
    edges = [s[f + atoms : f + size] for s, f in zip(slices, firsts)]
    near_grad = beside(jnp.stack([e[:face] for e in edges], axis=0), "slab", True)
    far_grad = inner(jnp.stack([e[face:] for e in edges], axis=0), "slab")
    near_sum = weight[0].astype(F32) + weight[1].astype(F32)
    weight = near_sum + (weight[2].astype(F32) + weight[3].astype(F32))
    columns = {0: weight}
    for bit in bits:
        arrived = {j ^ bit: partner(columns[j], "xy", bit) for j in columns}
        columns.update(arrived)
    mix_grad, gate_grad = call(
        functools.partial(assemble_kernel, plane),
        (
            jax.ShapeDtypeStruct((4, channels, channels), F32),
            jax.ShapeDtypeStruct((channels, 3 * channels), F32),
        ),
        [pltpu.VMEM((7, channels, channels), F32)],
        place,
        *[columns[j] for j in range(plane)],
    )
    mix_grad, gate_grad, near_grad, far_grad = lax.optimization_barrier((mix_grad, gate_grad, near_grad, far_grad))
    feat_grad = call(
        functools.partial(finish_kernel, plane, firsts),
        jax.ShapeDtypeStruct((atoms, harm_count, channels), F32),
        [],
        place,
        *slices,
        near_grad,
        far_grad,
        own,
        mix_weight,
        gate_weight,
    )
    return (density[0], feat_grad, mix_grad, gate_grad)


def solution(mesh):
    in_specs = (
        P(("slab", "xy"), None, None),
        P(),
        P(),
        P(),
        P(),
        P(None, None, ("slab", "xy")),
        P(None, ("slab", "xy")),
        P(("slab", "xy")),
        P(("slab", "xy")),
    )
    out_specs = (P(("slab", "xy")), P(("slab", "xy"), None, None), P(), P())
    return jax.shard_map(body, mesh=mesh, in_specs=in_specs, out_specs=out_specs, check_vma=False)
```

```python
import functools
import math

import jax
import jax.numpy as jnp
from jax import lax
from jax.experimental import pallas as pl
from jax.experimental.pallas import tpu as pltpu
from jax.sharding import PartitionSpec as P

DEGREE_SPANS = ((0, 1), (1, 4), (4, 9), (9, 16))
DEGREE_OF = (0,) + (1,) * 3 + (2,) * 5 + (3,) * 7
HARM = 16
SPACING = 0.35
root_three = math.sqrt(3.0)
cubic_outer = math.sqrt(10.0) / 4.0
cubic_middle = math.sqrt(15.0)
cubic_inner = math.sqrt(6.0) / 4.0
VMEM_BYTES = 20 * 2**20
F32 = jnp.float32
BF16 = jnp.bfloat16


def harmonics(x, y, z):
    r2 = x * x + y * y + z * z
    terms = [
        None,
        x,
        y,
        z,
        root_three * x * y,
        root_three * y * z,
        0.5 * (3.0 * z * z - r2),
        root_three * x * z,
        0.5 * root_three * (x * x - y * y),
        cubic_outer * y * (3.0 * x * x - y * y),
        cubic_middle * x * y * z,
        cubic_inner * y * (5.0 * z * z - r2),
        0.5 * z * (5.0 * z * z - 3.0 * r2),
        cubic_inner * x * (5.0 * z * z - r2),
        0.5 * cubic_middle * z * (x * x - y * y),
        cubic_outer * x * (x * x - 3.0 * y * y),
    ]
    return terms, r2


def split_high_low(values):
    high = values.astype(BF16)
    return high, (values - high.astype(F32)).astype(BF16)


def dot_lanes(left, right):
    return lax.dot_general(left, right, (((1,), (1,)), ((), ())), preferred_element_type=F32)


def dot(left, right):
    return jnp.dot(left, right, preferred_element_type=F32)


def partner(block, axis, bit):
    count = lax.axis_size(axis)
    return lax.ppermute(block, axis, [(i, i ^ bit) for i in range(count)])


def beside(block, first):
    slabs, plane = lax.axis_size("slab"), lax.axis_size("xy")
    route = []
    for slab in range(slabs):
        other = slab ^ 1 if first else ((slab + 1) ^ 1) - 1
        for j in range(plane):
            target = other * plane + j if 0 <= other < slabs else slab * plane + (j ^ 1)
            route.append((slab * plane + j, target))
    return lax.ppermute(block, ("slab", "xy"), route)


def table(column_ref, k, total):
    column = column_ref[k : k + 1, :]
    rows = lax.broadcasted_iota(jnp.int32, (total, column.shape[1]), 0)
    return jnp.where(rows == column, 1.0, 0.0).astype(BF16)


def pair_geometry(slots, atoms, edge, plane, place_ref, faces, lhs_ref, coef_ref, harm_ref, column_ref, target_ref):
    groups = (faces[0].shape[0] - 2 * HARM) // 3
    info = []
    for ref in faces:
        parts = [ref[2 * HARM + i * groups : 2 * HARM + (i + 1) * groups].astype(F32) for i in range(3)]
        info.append((parts[0] + parts[1] + parts[2]).reshape(groups * ref.shape[1], -1))

    def rows(first):
        return jnp.concatenate([x[first * slots : (first + 1) * slots, :] for x in info], axis=1)

    harm, r2 = harmonics(rows(0), rows(1), rows(2))
    for lm in range(1, HARM):
        harm_ref[lm * slots : (lm + 1) * slots, :] = harm[lm]
    harm_ref[:slots, :] = jnp.ones_like(r2)
    code = rows(3).astype(jnp.int32)
    tail = rows(4)
    target_ref[...] = tail
    slot = lax.broadcasted_iota(jnp.int32, code.shape, 0).astype(F32)
    active = (slot < tail[0:1, :]).astype(F32)
    relative = (code & (plane - 1)) ^ (place_ref[0] >> 1)
    offset = code >> (plane.bit_length() - 1)
    column_ref[...] = offset + relative * jnp.where(offset < plane * atoms, atoms, edge)
    envelope = (1.0 - r2 / 7.0) ** 2 * active
    distance = jnp.sqrt(r2)
    nbasis = lhs_ref.shape[1] // (3 * slots)
    values = [jnp.exp(-(((distance - SPACING * b) / SPACING) ** 2)) * envelope for b in range(nbasis)]
    high, low = split_high_low(jnp.concatenate(values, axis=0))
    coef_ref[...] = dot(lhs_ref[...], jnp.concatenate([high, low, high], axis=0))


def forward_kernel(slots, plane, place_ref, *refs):
    wide = refs[:plane]
    faces = refs[plane : 2 * plane]
    lhs_ref, mix_ref, gate_ref, out_w_ref = refs[2 * plane : 2 * plane + 4]
    feats_ref, mixed_ref, gates_ref, msg_ref, dens_ref = refs[2 * plane + 4 : 2 * plane + 9]
    coef_ref, harm_ref, column_ref, target_ref, source_ref = refs[2 * plane + 9 :]
    atoms = wide[0].shape[1]
    edge = (feats_ref.shape[1] - plane * atoms) // plane
    face = edge // 2
    total = plane * (atoms + edge)
    part = mix_ref.shape[1] // 2
    for j in range(plane):
        feats_ref[:, j * atoms : (j + 1) * atoms, :] = wide[j][...]
        for side in range(2):
            at = plane * atoms + j * edge + side * face
            feats_ref[:, at : at + face, :] = faces[j][side * HARM : (side + 1) * HARM]
    pair_geometry(slots, atoms, edge, plane, place_ref, faces, lhs_ref, coef_ref, harm_ref, column_ref, target_ref)
    gates_ref[...] = jax.nn.sigmoid(dot_lanes(gate_ref[...], feats_ref[0]))
    for lm in range(HARM):
        degree = DEGREE_OF[lm]
        both = dot_lanes(mix_ref[degree], feats_ref[lm])
        mixed, plain = both[:part], both[part:]
        mixed_ref[lm * part : (lm + 1) * part, :] = mixed
        if degree == 0:
            update = mixed * jax.nn.sigmoid(mixed)
        else:
            update = mixed * gates_ref[(degree - 1) * part : degree * part, :]
        source_ref[lm * part : (lm + 1) * part, :] = (plain + update).astype(BF16)
    message = jnp.zeros(msg_ref.shape, F32)
    for k in range(slots):
        rows = dot(source_ref[...], table(column_ref, k, total))
        for degree, (start, end) in enumerate(DEGREE_SPANS):
            inner = None
            for lm in range(start, end):
                term = rows[lm * part : (lm + 1) * part]
                if lm > 0:
                    term = term * harm_ref[lm * slots + k : lm * slots + k + 1, :]
                inner = term if inner is None else inner + term
            at = (k * 4 + degree) * part
            message = message + inner * coef_ref[at : at + part, :]
    msg_ref[...] = message
    partial = jnp.sum(message * jax.nn.sigmoid(message) * out_w_ref[...], axis=0, keepdims=True)
    dens_ref[...] = jnp.broadcast_to(partial, dens_ref.shape)


def backward_kernel(slots, plane, scale, probes_dev, *refs):
    dens = refs[:plane]
    coef_ref, harm_ref, column_ref, target_ref, feats_ref = refs[plane : plane + 5]
    mixed_ref, gates_ref, msg_ref, out_w_ref = refs[plane + 5 : plane + 9]
    weight_ref, density_ref = refs[plane + 9 : plane + 11]
    send_refs = refs[plane + 11 : -1]
    grad_ref = refs[-1]
    part = msg_ref.shape[0]
    total = feats_ref.shape[1]
    rows_out = send_refs[0].shape[0]
    atoms = 2 * rows_out // 3
    edge = rows_out - atoms
    probes = msg_ref.shape[1] // plane
    density = dens[0][0:1, :]
    for j in range(1, plane):
        other = dens[j][0:1, :]
        density = density + jnp.concatenate(
            [other[:, (b ^ j) * probes : ((b ^ j) + 1) * probes] for b in range(plane)], axis=1
        )
    density_ref[...] = jnp.broadcast_to(density[:, :probes], density_ref.shape)
    d_density = (density - target_ref[1:2, :]) * (1.0 / probes_dev)
    message = msg_ref[...]
    sig = jax.nn.sigmoid(message)
    d_message = d_density * out_w_ref[...] * (sig * (1.0 + message * (1.0 - sig)))
    for k in range(slots):
        pieces = []
        for degree, (start, end) in enumerate(DEGREE_SPANS):
            at = (k * 4 + degree) * part
            base = coef_ref[at : at + part, :] * d_message
            for lm in range(start, end):
                piece = base if lm == 0 else base * harm_ref[lm * slots + k : lm * slots + k + 1, :]
                pieces.append(piece.astype(BF16))
        contribution = jnp.concatenate(pieces, axis=0)
        product = dot_lanes(contribution, table(column_ref, k, total))
        if k == 0:
            grad_ref[...] = product
        else:
            grad_ref[...] += product
    for degree, (start, end) in enumerate(DEGREE_SPANS):
        sums = None
        gate_sum = None
        for lm in range(start, end):
            grad = grad_ref[lm * part : (lm + 1) * part, :]
            mixed = mixed_ref[lm * part : (lm + 1) * part, :]
            if degree == 0:
                s = jax.nn.sigmoid(mixed)
                d_mixed = grad * (s * (1.0 + mixed * (1.0 - s)))
            else:
                d_mixed = grad * gates_ref[(degree - 1) * part : degree * part, :]
                gate_sum = grad * mixed if gate_sum is None else gate_sum + grad * mixed
            high, low = split_high_low(d_mixed)
            product = dot(jnp.concatenate([high, low], axis=0), feats_ref[lm])
            sums = product if sums is None else sums + product
        weight_ref[degree * part : (degree + 1) * part, :] = (sums[:part] + sums[part:]) * scale
        if degree > 0:
            gates = gates_ref[(degree - 1) * part : degree * part, :]
            high, low = split_high_low(gate_sum * gates * (1.0 - gates))
            product = dot(jnp.concatenate([high, low], axis=0), feats_ref[0])
            at = (3 + degree) * part
            weight_ref[at : at + part, :] = (product[:part] + product[part:]) * scale
    turned = grad_ref[...].T
    for j in range(plane):
        send_ref = send_refs[j.bit_length()]
        first = (j - (1 << j.bit_length() >> 1)) * rows_out
        send_ref[first : first + atoms, :] = turned[j * atoms : (j + 1) * atoms].astype(BF16)
        at = plane * atoms + j * edge
        send_ref[first + atoms : first + rows_out, :] = turned[at : at + edge].astype(BF16)


def finish_kernel(plane, firsts, place_ref, *refs):
    slices = refs[:plane]
    near_ref, far_ref, feats_ref, mix_ref, gate_ref, out_ref = refs[plane:]
    atoms = feats_ref.shape[1]
    channels = feats_ref.shape[2]
    part = channels // plane
    face = near_ref.shape[1]
    odd = (jnp.zeros((face, channels), jnp.int32) + place_ref[0]) % 2 > 0
    per = channels // part
    me = place_ref[0] >> 1
    lane = lax.broadcasted_iota(jnp.int32, (atoms, channels), 1)
    gates = jax.nn.sigmoid(dot(feats_ref[0], gate_ref[...]))

    def slab(j, group):
        columns = slice(group * channels, (group + 1) * channels)
        own = slices[j][firsts[j] : firsts[j] + atoms, columns].astype(F32)
        near, far = near_ref[j, :, columns].astype(F32), far_ref[j, :, columns].astype(F32)
        low = own[:face] + jnp.where(odd, near, far)
        high = own[atoms - face :] + jnp.where(odd, far, near)
        return jnp.concatenate([low, own[face : atoms - face], high], axis=0)

    upstream = []
    for group in range(HARM // per):
        blocks = [slab(j, group) for j in range(plane)]
        for place in range(per):
            total = None
            for j in range(plane):
                home = (me ^ j) * part
                shift = (home - place * part + channels) % channels
                moved = pltpu.roll(blocks[j], shift, 1)
                keep = jnp.where((lane >= home) & (lane < home + part), moved, 0.0)
                total = keep if total is None else total + keep
            upstream.append(total)
    gate_parts = []
    zero_row = None
    for degree, (start, end) in enumerate(DEGREE_SPANS):
        weight = mix_ref[degree]
        mixed_all = dot(feats_ref[start:end].reshape(-1, channels), weight)
        gate_sum = None
        d_mixed = []
        for lm in range(start, end):
            mixed = mixed_all[(lm - start) * atoms : (lm - start + 1) * atoms]
            if degree == 0:
                s = jax.nn.sigmoid(mixed)
                d_mixed.append(upstream[lm] * (s * (1.0 + mixed * (1.0 - s))))
            else:
                d_mixed.append(upstream[lm] * gates[:, (degree - 1) * channels : degree * channels])
                product = upstream[lm] * mixed
                gate_sum = product if gate_sum is None else gate_sum + product
        high, low = split_high_low(jnp.concatenate(d_mixed, axis=0))
        rows = high.shape[0]
        back = dot_lanes(jnp.concatenate([high, low], axis=0), weight)
        back = back[:rows] + back[rows:]
        for lm in range(start, end):
            result = upstream[lm] + back[(lm - start) * atoms : (lm - start + 1) * atoms]
            if degree == 0:
                zero_row = result
            else:
                out_ref[:, lm, :] = result
        if degree > 0:
            gate_parts.append(gate_sum)
    d_gate = jnp.concatenate(gate_parts, axis=1) * gates * (1.0 - gates)
    high, low = split_high_low(d_gate)
    back = dot_lanes(jnp.concatenate([high, low], axis=0), gate_ref[...])
    out_ref[:, 0, :] = zero_row + back[:atoms] + back[atoms:]


def assemble_kernel(plane, place_ref, *refs):
    pieces = refs[:plane]
    mix_ref, gate_ref = refs[plane : plane + 2]
    (joined_ref,) = refs[plane + 2 :]
    part = pieces[0].shape[0] // 7
    channels = plane * part
    for j in range(plane):
        home = pl.multiple_of(((place_ref[0] >> 1) ^ j) * part, part)
        for block in range(7):
            joined_ref[block, pl.ds(home, part), :] = pieces[j][block * part : (block + 1) * part, :]
    for block in range(4):
        mix_ref[block] = joined_ref[block].T
    for block in range(3):
        gate_ref[:, block * channels : (block + 1) * channels] = joined_ref[4 + block].T


def call(kernel, outs, scratch, *arrays):
    vmem = pl.BlockSpec(memory_space=pltpu.VMEM)
    smem = pl.BlockSpec(memory_space=pltpu.SMEM)
    return pl.pallas_call(
        kernel,
        out_shape=outs,
        in_specs=[smem if x.shape == (1,) else vmem for x in arrays],
        out_specs=jax.tree.map(lambda _: vmem, outs),
        scratch_shapes=scratch,
        compiler_params=pltpu.CompilerParams(vmem_limit_bytes=VMEM_BYTES),
    )(*arrays)


def body(
    atom_feats,
    mix_weight,
    gate_weight,
    radial_weight,
    out_weight,
    pair_vec,
    nbr_atom,
    nbr_count,
    target,
):
    atoms, harm_count, channels = atom_feats.shape
    slots, probes = nbr_atom.shape
    nbasis = radial_weight.shape[0]
    plane = lax.axis_size("xy")
    slabs = lax.axis_size("slab")
    part = channels // plane
    face = atoms // 4
    edge = 2 * face
    total = plane * (atoms + edge)
    lanes = plane * probes
    me = lax.axis_index("xy").astype(jnp.int32)
    slab = lax.axis_index("slab").astype(jnp.int32)
    odd = slab % 2
    place = (me * 2 + odd)[None]

    domain = nbr_atom // atoms
    row = nbr_atom % atoms
    step = domain // plane - slab
    wide = plane * atoms
    below = wide + (1 - odd) * face + row - (atoms - face)
    above = wide + odd * face + row
    offset = jnp.where(step == 0, row, jnp.where(step < 0, below, above))
    code = offset * plane + domain % plane
    tail = jnp.concatenate(
        [nbr_count.astype(F32)[None], target[None], jnp.zeros((2 * slots - 2, probes), F32)], axis=0
    )
    info = jnp.concatenate([pair_vec.reshape(3 * slots, probes), code.astype(F32), tail], axis=0)

    own = jnp.transpose(atom_feats, (1, 0, 2))
    last = atoms - face
    near = beside(lax.dynamic_slice_in_dim(own, (1 - odd) * last, face, 1), True)
    far = beside(lax.dynamic_slice_in_dim(own, odd * last, face, 1), False)
    high = lax.reduce_precision(info, 8, 7)
    middle = lax.reduce_precision(info - high, 8, 7)
    parts = [x.astype(BF16) for x in (high, middle, info - high - middle)]
    faces = jnp.concatenate([near, far] + [x.reshape(-1, face, channels) for x in parts], axis=0)
    bits = [1 << b for b in reversed(range((plane - 1).bit_length()))]
    held = {0: (own, faces)}
    for bit in bits:
        for j in list(held):
            held[j ^ bit] = tuple(partner(x, "xy", bit) for x in held[j])
    pieces = [held[j] for j in range(plane)]

    first = me * part
    mix_part = lax.dynamic_slice_in_dim(mix_weight, first, part, axis=2)
    mix_part = jnp.transpose(mix_part, (0, 2, 1))
    pick = lax.broadcasted_iota(jnp.int32, (4, part, channels), 1) + first
    pick = (pick == lax.broadcasted_iota(jnp.int32, (4, part, channels), 2)).astype(BF16)
    mix_part = jnp.concatenate([mix_part, pick], axis=1)
    gate_part = lax.dynamic_slice_in_dim(gate_weight.reshape(channels, 3, channels), first, part, axis=2)
    gate_part = jnp.transpose(gate_part, (1, 2, 0)).reshape(3 * part, channels)
    radial_part = lax.dynamic_slice_in_dim(radial_weight.reshape(nbasis, 4, channels), first, part, axis=2)
    radial_part = jnp.transpose(radial_part, (1, 2, 0)).reshape(4 * part, nbasis)
    high = lax.reduce_precision(radial_part, 8, 7)
    three = jnp.stack([high, high, radial_part - high], axis=1)
    same = jnp.eye(slots, dtype=F32)
    radial_lhs = three[None, :, :, :, None] * same[:, None, None, None, :]
    radial_lhs = radial_lhs.reshape(slots * 4 * part, 3 * nbasis * slots).astype(BF16)
    out_part = lax.dynamic_slice_in_dim(out_weight, first, part)[:, None]

    feats, mixed, gates, message, dens, coef, harm, column, goals = call(
        functools.partial(forward_kernel, slots, plane),
        (
            jax.ShapeDtypeStruct((harm_count, total, channels), BF16),
            jax.ShapeDtypeStruct((harm_count * part, total), F32),
            jax.ShapeDtypeStruct((3 * part, total), F32),
            jax.ShapeDtypeStruct((part, lanes), F32),
            jax.ShapeDtypeStruct((8, lanes), F32),
            jax.ShapeDtypeStruct((slots * 4 * part, lanes), F32),
            jax.ShapeDtypeStruct((harm_count * slots, lanes), F32),
            jax.ShapeDtypeStruct((slots, lanes), jnp.int32),
            jax.ShapeDtypeStruct((slots, lanes), F32),
        ),
        [pltpu.VMEM((harm_count * part, total), BF16)],
        place,
        *[p[0] for p in pieces],
        *[p[1] for p in pieces],
        radial_lhs,
        mix_part,
        gate_part,
        out_part,
    )
    dens_all = [dens] + [partner(dens, "xy", j) for j in range(1, plane)]

    groups = [1] + [1 << b for b in range((plane - 1).bit_length())]
    outs = call(
        functools.partial(backward_kernel, slots, plane, 1.0 / float(slabs * plane), float(probes)),
        (
            jax.ShapeDtypeStruct((7 * part, channels), F32),
            jax.ShapeDtypeStruct((8, probes), F32),
        )
        + tuple(jax.ShapeDtypeStruct((rows * (atoms + edge), harm_count * part), BF16) for rows in groups),
        [pltpu.VMEM((harm_count * part, total), F32)],
        *dens_all,
        coef,
        harm,
        column,
        goals,
        feats,
        mixed,
        gates,
        message,
        out_part,
    )
    weight, density, sends = outs[0], outs[1], list(outs[2:])

    steps = [1 << b for b in range((slabs - 1).bit_length())]
    size = atoms + edge
    entries = [(0, sends[0], {0: 0})]
    for b, block in enumerate(sends[1:]):
        entries.append((0, block, {j: (j - (1 << b)) * size for j in range(1 << b, 2 << b)}))
    for bit in bits:
        due = [e for e in entries if any(bit <= j < 2 * bit for j in e[2])]
        for source, block, places in due:
            moved = {j ^ bit: at for j, at in places.items()}
            entries.append((source ^ bit, partner(block, "xy", bit), moved))
    mine = {source: (block, places[0]) for source, block, places in entries if 0 in places}
    slices = [mine[j][0] for j in range(plane)]
    firsts = tuple(mine[j][1] for j in range(plane))
    for bit in steps[:-2]:
        weight = weight + partner(weight, "slab", bit)
    weight = weight.astype(BF16)
    one, two = steps[-2:]
    weight = [weight] + [partner(weight, "slab", bit) for bit in (one, two, one + two)]
    *weight, last_slice = lax.optimization_barrier((*weight, slices[-1]))
    slices = slices[:-1] + [last_slice]
    edges = [s[f + atoms : f + size] for s, f in zip(slices, firsts)]
    near_grad = beside(jnp.stack([e[:face] for e in edges], axis=0), True)
    far_grad = beside(jnp.stack([e[face:] for e in edges], axis=0), False)
    near_sum = weight[0].astype(F32) + weight[1].astype(F32)
    weight = near_sum + (weight[2].astype(F32) + weight[3].astype(F32))
    columns = {0: weight}
    for bit in bits:
        arrived = {j ^ bit: partner(columns[j], "xy", bit) for j in columns}
        columns.update(arrived)
    mix_grad, gate_grad = call(
        functools.partial(assemble_kernel, plane),
        (
            jax.ShapeDtypeStruct((4, channels, channels), F32),
            jax.ShapeDtypeStruct((channels, 3 * channels), F32),
        ),
        [pltpu.VMEM((7, channels, channels), F32)],
        place,
        *[columns[j] for j in range(plane)],
    )
    mix_grad, gate_grad, near_grad, far_grad = lax.optimization_barrier((mix_grad, gate_grad, near_grad, far_grad))
    feat_grad = call(
        functools.partial(finish_kernel, plane, firsts),
        jax.ShapeDtypeStruct((atoms, harm_count, channels), F32),
        [],
        place,
        *slices,
        near_grad,
        far_grad,
        own,
        mix_weight,
        gate_weight,
    )
    return (density[0], feat_grad, mix_grad, gate_grad)


def solution(mesh):
    in_specs = (
        P(("slab", "xy"), None, None),
        P(),
        P(),
        P(),
        P(),
        P(None, None, ("slab", "xy")),
        P(None, ("slab", "xy")),
        P(("slab", "xy")),
        P(("slab", "xy")),
    )
    out_specs = (P(("slab", "xy")), P(("slab", "xy"), None, None), P(), P())
    return jax.shard_map(body, mesh=mesh, in_specs=in_specs, out_specs=out_specs, check_vma=False)
```

```python
import functools
import math

import jax
import jax.numpy as jnp
from jax import lax
from jax.experimental import pallas as pl
from jax.experimental.pallas import tpu as pltpu
from jax.sharding import PartitionSpec as P

DEGREE_SPANS = ((0, 1), (1, 4), (4, 9), (9, 16))
DEGREE_OF = (0,) + (1,) * 3 + (2,) * 5 + (3,) * 7
HARM = 16
SPACING = 0.35
root_three = math.sqrt(3.0)
cubic_outer = math.sqrt(10.0) / 4.0
cubic_middle = math.sqrt(15.0)
cubic_inner = math.sqrt(6.0) / 4.0
VMEM_BYTES = 20 * 2**20
F32 = jnp.float32
BF16 = jnp.bfloat16


def harmonics(x, y, z):
    r2 = x * x + y * y + z * z
    terms = [
        None,
        x,
        y,
        z,
        root_three * x * y,
        root_three * y * z,
        0.5 * (3.0 * z * z - r2),
        root_three * x * z,
        0.5 * root_three * (x * x - y * y),
        cubic_outer * y * (3.0 * x * x - y * y),
        cubic_middle * x * y * z,
        cubic_inner * y * (5.0 * z * z - r2),
        0.5 * z * (5.0 * z * z - 3.0 * r2),
        cubic_inner * x * (5.0 * z * z - r2),
        0.5 * cubic_middle * z * (x * x - y * y),
        cubic_outer * x * (x * x - 3.0 * y * y),
    ]
    return terms, r2


def split_high_low(values):
    high = values.astype(BF16)
    return high, (values - high.astype(F32)).astype(BF16)


def dot_lanes(left, right):
    return lax.dot_general(left, right, (((1,), (1,)), ((), ())), preferred_element_type=F32)


def dot(left, right):
    return jnp.dot(left, right, preferred_element_type=F32)


def partner(block, axis, bit):
    count = lax.axis_size(axis)
    return lax.ppermute(block, axis, [(i, i ^ bit) for i in range(count)])


def beside(block, first):
    slabs, plane = lax.axis_size("slab"), lax.axis_size("xy")
    route = []
    for slab in range(slabs):
        other = slab ^ 1 if first else ((slab + 1) ^ 1) - 1
        for j in range(plane):
            target = other * plane + j if 0 <= other < slabs else slab * plane + (j ^ 1)
            route.append((slab * plane + j, target))
    return lax.ppermute(block, ("slab", "xy"), route)


def table(column_ref, k, total):
    column = column_ref[k : k + 1, :]
    rows = lax.broadcasted_iota(jnp.int32, (total, column.shape[1]), 0)
    return jnp.where(rows == column, 1.0, 0.0).astype(BF16)


def pair_geometry(slots, atoms, edge, plane, place_ref, faces, lhs_ref, coef_ref, harm_ref, column_ref, target_ref):
    groups = (faces[0].shape[0] - 2 * HARM) // 3
    info = []
    for ref in faces:
        parts = [ref[2 * HARM + i * groups : 2 * HARM + (i + 1) * groups].astype(F32) for i in range(3)]
        info.append((parts[0] + parts[1] + parts[2]).reshape(groups * ref.shape[1], -1))

    def rows(first):
        return jnp.concatenate([x[first * slots : (first + 1) * slots, :] for x in info], axis=1)

    harm, r2 = harmonics(rows(0), rows(1), rows(2))
    for lm in range(1, HARM):
        harm_ref[lm * slots : (lm + 1) * slots, :] = harm[lm]
    harm_ref[:slots, :] = jnp.ones_like(r2)
    code = rows(3).astype(jnp.int32)
    tail = rows(4)
    target_ref[...] = tail
    slot = lax.broadcasted_iota(jnp.int32, code.shape, 0).astype(F32)
    active = (slot < tail[0:1, :]).astype(F32)
    relative = (code & (plane - 1)) ^ (place_ref[0] >> 1)
    offset = code >> (plane.bit_length() - 1)
    column_ref[...] = offset + relative * jnp.where(offset < plane * atoms, atoms, edge)
    envelope = (1.0 - r2 / 7.0) ** 2 * active
    distance = jnp.sqrt(r2)
    nbasis = lhs_ref.shape[1] // (3 * slots)
    values = [jnp.exp(-(((distance - SPACING * b) / SPACING) ** 2)) * envelope for b in range(nbasis)]
    high, low = split_high_low(jnp.concatenate(values, axis=0))
    coef_ref[...] = dot(lhs_ref[...], jnp.concatenate([high, low, high], axis=0))


def forward_kernel(slots, plane, place_ref, *refs):
    wide = refs[:plane]
    faces = refs[plane : 2 * plane]
    lhs_ref, mix_ref, gate_ref, out_w_ref = refs[2 * plane : 2 * plane + 4]
    feats_ref, mixed_ref, gates_ref, msg_ref, dens_ref = refs[2 * plane + 4 : 2 * plane + 9]
    coef_ref, harm_ref, column_ref, target_ref, source_ref = refs[2 * plane + 9 :]
    atoms = wide[0].shape[1]
    edge = (feats_ref.shape[1] - plane * atoms) // plane
    face = edge // 2
    total = plane * (atoms + edge)
    part = mix_ref.shape[1] // 2
    for j in range(plane):
        feats_ref[:, j * atoms : (j + 1) * atoms, :] = wide[j][...]
        for side in range(2):
            at = plane * atoms + j * edge + side * face
            feats_ref[:, at : at + face, :] = faces[j][side * HARM : (side + 1) * HARM]
    pair_geometry(slots, atoms, edge, plane, place_ref, faces, lhs_ref, coef_ref, harm_ref, column_ref, target_ref)
    gates_ref[...] = jax.nn.sigmoid(dot_lanes(gate_ref[...], feats_ref[0]))
    for lm in range(HARM):
        degree = DEGREE_OF[lm]
        both = dot_lanes(mix_ref[degree], feats_ref[lm])
        mixed, plain = both[:part], both[part:]
        mixed_ref[lm * part : (lm + 1) * part, :] = mixed
        if degree == 0:
            update = mixed * jax.nn.sigmoid(mixed)
        else:
            update = mixed * gates_ref[(degree - 1) * part : degree * part, :]
        source_ref[lm * part : (lm + 1) * part, :] = (plain + update).astype(BF16)
    message = jnp.zeros(msg_ref.shape, F32)
    for k in range(slots):
        rows = dot(source_ref[...], table(column_ref, k, total))
        for degree, (start, end) in enumerate(DEGREE_SPANS):
            inner = None
            for lm in range(start, end):
                term = rows[lm * part : (lm + 1) * part]
                if lm > 0:
                    term = term * harm_ref[lm * slots + k : lm * slots + k + 1, :]
                inner = term if inner is None else inner + term
            at = (k * 4 + degree) * part
            message = message + inner * coef_ref[at : at + part, :]
    msg_ref[...] = message
    partial = jnp.sum(message * jax.nn.sigmoid(message) * out_w_ref[...], axis=0, keepdims=True)
    dens_ref[...] = partial


def backward_kernel(slots, plane, scale, probes_dev, *refs):
    dens = refs[:plane]
    coef_ref, harm_ref, column_ref, target_ref, feats_ref = refs[plane : plane + 5]
    mixed_ref, gates_ref, msg_ref, out_w_ref = refs[plane + 5 : plane + 9]
    weight_ref, density_ref = refs[plane + 9 : plane + 11]
    send_refs = refs[plane + 11 : -1]
    grad_ref = refs[-1]
    part = msg_ref.shape[0]
    total = feats_ref.shape[1]
    rows_out = send_refs[0].shape[0]
    atoms = 2 * rows_out // 3
    edge = rows_out - atoms
    probes = msg_ref.shape[1] // plane
    density = dens[0][0:1, :]
    for j in range(1, plane):
        other = dens[j][0:1, :]
        density = density + jnp.concatenate(
            [other[:, (b ^ j) * probes : ((b ^ j) + 1) * probes] for b in range(plane)], axis=1
        )
    density_ref[...] = jnp.broadcast_to(density[:, :probes], density_ref.shape)
    d_density = (density - target_ref[1:2, :]) * (1.0 / probes_dev)
    message = msg_ref[...]
    sig = jax.nn.sigmoid(message)
    d_message = d_density * out_w_ref[...] * (sig * (1.0 + message * (1.0 - sig)))
    for k in range(slots):
        pieces = []
        for degree, (start, end) in enumerate(DEGREE_SPANS):
            at = (k * 4 + degree) * part
            base = coef_ref[at : at + part, :] * d_message
            for lm in range(start, end):
                piece = base if lm == 0 else base * harm_ref[lm * slots + k : lm * slots + k + 1, :]
                pieces.append(piece.astype(BF16))
        contribution = jnp.concatenate(pieces, axis=0)
        product = dot_lanes(contribution, table(column_ref, k, total))
        if k == 0:
            grad_ref[...] = product
        else:
            grad_ref[...] += product
    for degree, (start, end) in enumerate(DEGREE_SPANS):
        sums = None
        gate_sum = None
        for lm in range(start, end):
            grad = grad_ref[lm * part : (lm + 1) * part, :]
            mixed = mixed_ref[lm * part : (lm + 1) * part, :]
            if degree == 0:
                s = jax.nn.sigmoid(mixed)
                d_mixed = grad * (s * (1.0 + mixed * (1.0 - s)))
            else:
                d_mixed = grad * gates_ref[(degree - 1) * part : degree * part, :]
                gate_sum = grad * mixed if gate_sum is None else gate_sum + grad * mixed
            high, low = split_high_low(d_mixed)
            product = dot(jnp.concatenate([high, low], axis=0), feats_ref[lm])
            sums = product if sums is None else sums + product
        weight_ref[degree * part : (degree + 1) * part, :] = (sums[:part] + sums[part:]) * scale
        if degree > 0:
            gates = gates_ref[(degree - 1) * part : degree * part, :]
            high, low = split_high_low(gate_sum * gates * (1.0 - gates))
            product = dot(jnp.concatenate([high, low], axis=0), feats_ref[0])
            at = (3 + degree) * part
            weight_ref[at : at + part, :] = (product[:part] + product[part:]) * scale
    turned = grad_ref[...].T
    for j in range(plane):
        send_ref = send_refs[j.bit_length()]
        first = (j - (1 << j.bit_length() >> 1)) * rows_out
        send_ref[first : first + atoms, :] = turned[j * atoms : (j + 1) * atoms].astype(BF16)
        at = plane * atoms + j * edge
        send_ref[first + atoms : first + rows_out, :] = turned[at : at + edge].astype(BF16)


def finish_kernel(plane, firsts, place_ref, *refs):
    slices = refs[:plane]
    near_ref, far_ref, feats_ref, mix_ref, gate_ref, out_ref = refs[plane:]
    atoms = feats_ref.shape[1]
    channels = feats_ref.shape[2]
    part = channels // plane
    face = near_ref.shape[1]
    odd = (jnp.zeros((face, channels), jnp.int32) + place_ref[0]) % 2 > 0
    per = channels // part
    me = place_ref[0] >> 1
    lane = lax.broadcasted_iota(jnp.int32, (atoms, channels), 1)
    gates = jax.nn.sigmoid(dot(feats_ref[0], gate_ref[...]))

    def slab(j, group):
        columns = slice(group * channels, (group + 1) * channels)
        own = slices[j][firsts[j] : firsts[j] + atoms, columns].astype(F32)
        near, far = near_ref[j, :, columns].astype(F32), far_ref[j, :, columns].astype(F32)
        low = own[:face] + jnp.where(odd, near, far)
        high = own[atoms - face :] + jnp.where(odd, far, near)
        return jnp.concatenate([low, own[face : atoms - face], high], axis=0)

    upstream = []
    for group in range(HARM // per):
        blocks = [slab(j, group) for j in range(plane)]
        for place in range(per):
            total = None
            for j in range(plane):
                home = (me ^ j) * part
                shift = (home - place * part + channels) % channels
                moved = pltpu.roll(blocks[j], shift, 1)
                keep = jnp.where((lane >= home) & (lane < home + part), moved, 0.0)
                total = keep if total is None else total + keep
            upstream.append(total)
    gate_parts = []
    zero_row = None
    for degree, (start, end) in enumerate(DEGREE_SPANS):
        weight = mix_ref[degree]
        mixed_all = dot(feats_ref[start:end].reshape(-1, channels), weight)
        gate_sum = None
        d_mixed = []
        for lm in range(start, end):
            mixed = mixed_all[(lm - start) * atoms : (lm - start + 1) * atoms]
            if degree == 0:
                s = jax.nn.sigmoid(mixed)
                d_mixed.append(upstream[lm] * (s * (1.0 + mixed * (1.0 - s))))
            else:
                d_mixed.append(upstream[lm] * gates[:, (degree - 1) * channels : degree * channels])
                product = upstream[lm] * mixed
                gate_sum = product if gate_sum is None else gate_sum + product
        high, low = split_high_low(jnp.concatenate(d_mixed, axis=0))
        rows = high.shape[0]
        back = dot_lanes(jnp.concatenate([high, low], axis=0), weight)
        back = back[:rows] + back[rows:]
        for lm in range(start, end):
            result = upstream[lm] + back[(lm - start) * atoms : (lm - start + 1) * atoms]
            if degree == 0:
                zero_row = result
            else:
                out_ref[:, lm, :] = result
        if degree > 0:
            gate_parts.append(gate_sum)
    d_gate = jnp.concatenate(gate_parts, axis=1) * gates * (1.0 - gates)
    high, low = split_high_low(d_gate)
    back = dot_lanes(jnp.concatenate([high, low], axis=0), gate_ref[...])
    out_ref[:, 0, :] = zero_row + back[:atoms] + back[atoms:]


def assemble_kernel(plane, place_ref, *refs):
    pieces = refs[:plane]
    mix_ref, gate_ref = refs[plane : plane + 2]
    (joined_ref,) = refs[plane + 2 :]
    part = pieces[0].shape[0] // 7
    channels = plane * part
    for j in range(plane):
        home = pl.multiple_of(((place_ref[0] >> 1) ^ j) * part, part)
        for block in range(7):
            joined_ref[block, pl.ds(home, part), :] = pieces[j][block * part : (block + 1) * part, :]
    for block in range(4):
        mix_ref[block] = joined_ref[block].T
    for block in range(3):
        gate_ref[:, block * channels : (block + 1) * channels] = joined_ref[4 + block].T


def call(kernel, outs, scratch, *arrays):
    vmem = pl.BlockSpec(memory_space=pltpu.VMEM)
    smem = pl.BlockSpec(memory_space=pltpu.SMEM)
    return pl.pallas_call(
        kernel,
        out_shape=outs,
        in_specs=[smem if x.shape == (1,) else vmem for x in arrays],
        out_specs=jax.tree.map(lambda _: vmem, outs),
        scratch_shapes=scratch,
        compiler_params=pltpu.CompilerParams(vmem_limit_bytes=VMEM_BYTES),
    )(*arrays)


def body(
    atom_feats,
    mix_weight,
    gate_weight,
    radial_weight,
    out_weight,
    pair_vec,
    nbr_atom,
    nbr_count,
    target,
):
    atoms, harm_count, channels = atom_feats.shape
    slots, probes = nbr_atom.shape
    nbasis = radial_weight.shape[0]
    plane = lax.axis_size("xy")
    slabs = lax.axis_size("slab")
    part = channels // plane
    face = atoms // 4
    edge = 2 * face
    total = plane * (atoms + edge)
    lanes = plane * probes
    me = lax.axis_index("xy").astype(jnp.int32)
    slab = lax.axis_index("slab").astype(jnp.int32)
    odd = slab % 2
    place = (me * 2 + odd)[None]

    domain = nbr_atom // atoms
    row = nbr_atom % atoms
    step = domain // plane - slab
    wide = plane * atoms
    below = wide + (1 - odd) * face + row - (atoms - face)
    above = wide + odd * face + row
    offset = jnp.where(step == 0, row, jnp.where(step < 0, below, above))
    code = offset * plane + domain % plane
    tail = jnp.concatenate(
        [nbr_count.astype(F32)[None], target[None], jnp.zeros((2 * slots - 2, probes), F32)], axis=0
    )
    info = jnp.concatenate([pair_vec.reshape(3 * slots, probes), code.astype(F32), tail], axis=0)

    own = jnp.transpose(atom_feats, (1, 0, 2))
    last = atoms - face
    near = beside(lax.dynamic_slice_in_dim(own, (1 - odd) * last, face, 1), True)
    far = beside(lax.dynamic_slice_in_dim(own, odd * last, face, 1), False)
    high = lax.reduce_precision(info, 8, 7)
    middle = lax.reduce_precision(info - high, 8, 7)
    parts = [x.astype(BF16) for x in (high, middle, info - high - middle)]
    faces = jnp.concatenate([near, far] + [x.reshape(-1, face, channels) for x in parts], axis=0)
    bits = [1 << b for b in reversed(range((plane - 1).bit_length()))]
    held = {0: (own, faces)}
    for bit in bits:
        for j in list(held):
            held[j ^ bit] = tuple(partner(x, "xy", bit) for x in held[j])
    pieces = [held[j] for j in range(plane)]

    first = me * part
    mix_part = lax.dynamic_slice_in_dim(mix_weight, first, part, axis=2)
    mix_part = jnp.transpose(mix_part, (0, 2, 1))
    pick = lax.broadcasted_iota(jnp.int32, (4, part, channels), 1) + first
    pick = (pick == lax.broadcasted_iota(jnp.int32, (4, part, channels), 2)).astype(BF16)
    mix_part = jnp.concatenate([mix_part, pick], axis=1)
    gate_part = lax.dynamic_slice_in_dim(gate_weight.reshape(channels, 3, channels), first, part, axis=2)
    gate_part = jnp.transpose(gate_part, (1, 2, 0)).reshape(3 * part, channels)
    radial_part = lax.dynamic_slice_in_dim(radial_weight.reshape(nbasis, 4, channels), first, part, axis=2)
    radial_part = jnp.transpose(radial_part, (1, 2, 0)).reshape(4 * part, nbasis)
    high = lax.reduce_precision(radial_part, 8, 7)
    three = jnp.stack([high, high, radial_part - high], axis=1)
    same = jnp.eye(slots, dtype=F32)
    radial_lhs = three[None, :, :, :, None] * same[:, None, None, None, :]
    radial_lhs = radial_lhs.reshape(slots * 4 * part, 3 * nbasis * slots).astype(BF16)
    out_part = lax.dynamic_slice_in_dim(out_weight, first, part)[:, None]

    feats, mixed, gates, message, dens, coef, harm, column, goals = call(
        functools.partial(forward_kernel, slots, plane),
        (
            jax.ShapeDtypeStruct((harm_count, total, channels), BF16),
            jax.ShapeDtypeStruct((harm_count * part, total), F32),
            jax.ShapeDtypeStruct((3 * part, total), F32),
            jax.ShapeDtypeStruct((part, lanes), F32),
            jax.ShapeDtypeStruct((1, lanes), F32),
            jax.ShapeDtypeStruct((slots * 4 * part, lanes), F32),
            jax.ShapeDtypeStruct((harm_count * slots, lanes), F32),
            jax.ShapeDtypeStruct((slots, lanes), jnp.int32),
            jax.ShapeDtypeStruct((slots, lanes), F32),
        ),
        [pltpu.VMEM((harm_count * part, total), BF16)],
        place,
        *[p[0] for p in pieces],
        *[p[1] for p in pieces],
        radial_lhs,
        mix_part,
        gate_part,
        out_part,
    )
    dens_all = [dens] + [partner(dens, "xy", j) for j in range(1, plane)]

    groups = [1] + [1 << b for b in range((plane - 1).bit_length())]
    outs = call(
        functools.partial(backward_kernel, slots, plane, 1.0 / float(slabs * plane), float(probes)),
        (
            jax.ShapeDtypeStruct((7 * part, channels), F32),
            jax.ShapeDtypeStruct((8, probes), F32),
        )
        + tuple(jax.ShapeDtypeStruct((rows * (atoms + edge), harm_count * part), BF16) for rows in groups),
        [pltpu.VMEM((harm_count * part, total), F32)],
        *dens_all,
        coef,
        harm,
        column,
        goals,
        feats,
        mixed,
        gates,
        message,
        out_part,
    )
    weight, density, sends = outs[0], outs[1], list(outs[2:])

    steps = [1 << b for b in range((slabs - 1).bit_length())]
    size = atoms + edge
    entries = [(0, sends[0], {0: 0})]
    for b, block in enumerate(sends[1:]):
        entries.append((0, block, {j: (j - (1 << b)) * size for j in range(1 << b, 2 << b)}))
    for bit in bits:
        due = [e for e in entries if any(bit <= j < 2 * bit for j in e[2])]
        for source, block, places in due:
            moved = {j ^ bit: at for j, at in places.items()}
            entries.append((source ^ bit, partner(block, "xy", bit), moved))
    mine = {source: (block, places[0]) for source, block, places in entries if 0 in places}
    slices = [mine[j][0] for j in range(plane)]
    firsts = tuple(mine[j][1] for j in range(plane))
    for bit in steps[:-2]:
        weight = weight + partner(weight, "slab", bit)
    weight = weight.astype(BF16)
    one, two = steps[-2:]
    weight = [weight] + [partner(weight, "slab", bit) for bit in (one, two, one + two)]
    *weight, last_slice = lax.optimization_barrier((*weight, slices[-1]))
    slices = slices[:-1] + [last_slice]
    edges = [s[f + atoms : f + size] for s, f in zip(slices, firsts)]
    near_grad = beside(jnp.stack([e[:face] for e in edges], axis=0), True)
    far_grad = beside(jnp.stack([e[face:] for e in edges], axis=0), False)
    near_sum = weight[0].astype(F32) + weight[1].astype(F32)
    weight = near_sum + (weight[2].astype(F32) + weight[3].astype(F32))
    columns = {0: weight}
    for bit in bits:
        arrived = {j ^ bit: partner(columns[j], "xy", bit) for j in columns}
        columns.update(arrived)
    mix_grad, gate_grad = call(
        functools.partial(assemble_kernel, plane),
        (
            jax.ShapeDtypeStruct((4, channels, channels), F32),
            jax.ShapeDtypeStruct((channels, 3 * channels), F32),
        ),
        [pltpu.VMEM((7, channels, channels), F32)],
        place,
        *[columns[j] for j in range(plane)],
    )
    mix_grad, gate_grad, near_grad, far_grad = lax.optimization_barrier((mix_grad, gate_grad, near_grad, far_grad))
    feat_grad = call(
        functools.partial(finish_kernel, plane, firsts),
        jax.ShapeDtypeStruct((atoms, harm_count, channels), F32),
        [],
        place,
        *slices,
        near_grad,
        far_grad,
        own,
        mix_weight,
        gate_weight,
    )
    return (density[0], feat_grad, mix_grad, gate_grad)


def solution(mesh):
    in_specs = (
        P(("slab", "xy"), None, None),
        P(),
        P(),
        P(),
        P(),
        P(None, None, ("slab", "xy")),
        P(None, ("slab", "xy")),
        P(("slab", "xy")),
        P(("slab", "xy")),
    )
    out_specs = (P(("slab", "xy")), P(("slab", "xy"), None, None), P(), P())
    return jax.shard_map(body, mesh=mesh, in_specs=in_specs, out_specs=out_specs, check_vma=False)
```
